512 devices in a mesh: seq: 128 (over z, y_lo, x), chan: 4 (over y_hi, core).
Axes of the slice: x: 4, y: 8 (y_hi: 2, y_lo: 4; y = y_hi * 4 + y_lo), z: 8, core: 2. Of those that a mesh axis runs over, the one named last changes fastest.
Arguments:
- inputs: bfloat16 [2, 960, 32768], P(None, 'chan', 'seq'), may hold values from -6 to 6
- first_blocks: bfloat16 [256, 128, 128], P('seq'), may hold values from -0.5 to 0.5
- second_blocks: bfloat16 [128, 256, 256], P('seq'), may hold values from -0.375 to 0.375
- kernel: float32 [3, 960], P(None, 'chan'), may hold values from -3 to 3
- cotangent: bfloat16 [2, 960, 32768], P(None, 'chan', 'seq'), may hold values from -6 to 6
Outputs:
- mixed: bfloat16 [2, 960, 32768], P(None, 'chan', 'seq')
- input_grad: bfloat16 [2, 960, 32768], P(None, 'chan', 'seq')
- kernel_grad: float32 [3, 960], P(None, 'chan')
- block_grad: float32 [256, 128, 128], P('seq', 'chan')
- factor_grad: float32 [128, 256, 256], P('seq', 'chan')
The draws below stay inside these ranges and needn't reach their ends.
All inputs are finite; a program needn't handle non-finite values.
Results may differ from the reference program's by a relative error of at most 0.007.
Values may be sent and summed in bfloat16 or wider, within the bound.
A program may use at most 64 MiB of HBM per device.

```python
import jax
import jax.numpy as jnp

C = 960
BLK = 128
KW = 3
BATCH = 2
Q = 256
LEN = 32768


def block_scale(own_key, shape, pieces, smallest, largest):
    loudness = 1.0
    for position, parts in pieces:
        heights = jax.random.uniform(jax.random.fold_in(jax.random.fold_in(own_key, 6), position), (parts,), jnp.float32, smallest / len(pieces), largest / len(pieces))
        loudness = loudness * jnp.repeat(jnp.exp(heights), shape[position] // parts).reshape((-1,) + (1,) * (len(shape) - 1 - position))
    return loudness


def centred(rng, dims, scale, bound, cuts=(), kind=jnp.bfloat16):
    drawn = jax.random.normal(rng, dims, jnp.float32) * scale
    if len(cuts) > 0:
        drawn = block_scale(rng, dims, cuts, -0.22, 0.18) * drawn
    return jnp.clip(drawn, min=-bound, max=bound).astype(kind)


def setup_inputs(seed: int = 0) -> dict:
    arg_keys = jax.random.split(jax.random.key(seed), 6)
    inputs = centred(arg_keys[0], (BATCH, C, LEN), 1.0, 6.0, ((1, 4), (2, 128)))
    first_blocks = centred(arg_keys[1], (Q, BLK, BLK), BLK ** -0.5, 0.5, ((0, 128),))
    second_blocks = centred(arg_keys[2], (BLK, Q, Q), Q ** -0.5, 0.375, ((0, 128),))
    kernel = centred(arg_keys[3], (KW, C), 0.6, 3.0, ((1, 4),), jnp.float32)
    cotangent = centred(arg_keys[4], (BATCH, C, LEN), 1.0, 6.0, ((1, 4), (2, 128)))
    return dict(inputs=inputs, first_blocks=first_blocks, second_blocks=second_blocks, kernel=kernel, cotangent=cotangent)


def one_sequence(inputs, first_blocks, second_blocks, kernel, cotangent):
    channels, length = inputs.shape
    block_count = length // BLK
    tap_count = kernel.shape[0]
    in_float = inputs.astype(jnp.float32)
    blocked = in_float.reshape(channels, block_count, BLK)
    first_float = first_blocks.astype(jnp.float32)
    second_float = second_blocks.astype(jnp.float32)
    mixed_in = jnp.einsum('cqp,qpr->crq', blocked, first_float).astype(jnp.bfloat16)
    factor_out = jnp.einsum('cpq,pqk->cpk', mixed_in.astype(jnp.float32), second_float).astype(jnp.bfloat16)
    monarch = jnp.swapaxes(factor_out, 1, 2).reshape(channels, length).astype(jnp.float32)
    gated = (in_float * monarch).astype(jnp.bfloat16)
    gated_float = gated.astype(jnp.float32)
    padded = jnp.pad(gated_float, ((0, 0), (tap_count - 1, 0)))
    total = jnp.zeros((channels, length), jnp.float32)
    for tap_index in range(tap_count):
        start = tap_count - 1 - tap_index
        total = total + kernel[tap_index][:, None] * padded[:, start:start + length]
    mixed = total.astype(jnp.bfloat16)
    extended = jnp.pad(cotangent.astype(jnp.float32), ((0, 0), (0, tap_count - 1)))
    gate_grad = jnp.zeros((channels, length), jnp.float32)
    kernel_rows = []
    for tap_index in range(tap_count):
        window = extended[:, tap_index:tap_index + length]
        gate_grad = gate_grad + kernel[tap_index][:, None] * window
        kernel_rows.append(jnp.sum(gated_float * window, axis=1))
    kernel_grad = jnp.stack(kernel_rows)
    direct = gate_grad * monarch
    monarch_grad = (gate_grad * in_float).astype(jnp.bfloat16)
    adjoint = jnp.swapaxes(monarch_grad.astype(jnp.float32).reshape(channels, block_count, BLK), 1, 2)
    mixed_grad = jnp.einsum('cpk,pqk->cpq', adjoint, second_float).astype(jnp.bfloat16).astype(jnp.float32)
    through = jnp.einsum('crq,qpr->cqp', mixed_grad, first_float).reshape(channels, length)
    input_grad = (direct + through).astype(jnp.bfloat16)
    block_grad = jnp.einsum('cqp,crq->qpr', blocked, mixed_grad)
    factor_grad = jnp.einsum('cpq,cpk->pqk', mixed_in.astype(jnp.float32), adjoint)
    return mixed, input_grad, kernel_grad, block_grad, factor_grad


def reference(inputs, first_blocks, second_blocks, kernel, cotangent):
    mixed_rows = []
    grad_rows = []
    kernel_grad = jnp.zeros(kernel.shape, jnp.float32)
    block_grad = jnp.zeros(first_blocks.shape, jnp.float32)
    factor_grad = jnp.zeros(second_blocks.shape, jnp.float32)
    for item in range(inputs.shape[0]):
        result = one_sequence(inputs[item], first_blocks, second_blocks, kernel, cotangent[item])
        mixed_rows.append(result[0])
        grad_rows.append(result[1])
        kernel_grad = kernel_grad + result[2]
        block_grad = block_grad + result[3]
        factor_grad = factor_grad + result[4]
    return jnp.stack(mixed_rows), jnp.stack(grad_rows), kernel_grad, block_grad, factor_grad
```

```python
import jax
import jax.numpy as jnp
from jax import lax
from jax.experimental import pallas as pl
from jax.experimental.pallas import tpu as pltpu
from jax.sharding import PartitionSpec as P

NX, NL = 8, 16
SEQ, CHAN = NX * NL, 4
BATCH, CH, EXT, BLK = 2, 240, 256, 128
ROWS = BATCH * CH
LANES = 512
MESH = pl.DeviceIdType.MESH
BF, F32 = jnp.bfloat16, jnp.float32


def dot(a, b, ca, cb):
    return lax.dot_general(a, b, (((ca,), (cb,)), ((), ())), preferred_element_type=F32)


def nn(a, b):
    return dot(a, b, 1, 0)


def nt(a, b):
    return dot(a, b, 1, 1)


def tn(a, b):
    return dot(a, b, 0, 0)


def hot(shape, where):
    row = lax.broadcasted_iota(jnp.int32, shape, 0)
    col = lax.broadcasted_iota(jnp.int32, shape, 1)
    return jnp.where(where(row, col), 1.0, 0.0).astype(BF)


def place0(r, c):
    return ((r >> 4) & 1) * 128 + (r & 15) * 8 + (r >> 5) == c


def turn0(r, c):
    return ((r >> 1) & 7) * 32 + (r & 1) * 16 + (r >> 4) == c


def place1(r, c):
    return ((r >> 3) & 1) * 128 + (r >> 4) * 8 + (r & 7) == c


def turn1(r, c):
    return ((r >> 1) & 15) * 16 + (r & 1) * 8 + (r >> 5) == c


def order1(r, c):
    return ((r >> 1) & 7) * 32 + (r >> 4) * 2 + (r & 1) == c


def flip(where):
    return lambda r, c: where(c, r)


def body(
    x_ref, f_ref, s_ref, k_ref, c_ref,
    mixed_ref, igrad_ref, kgrad_ref, bgrad_ref, fgrad_ref,
    xs, cs, xt, gate, kpad, kcol, prod_w, st, s11, mgr,
    a0s, a0r, b0s, b0r, b1s, b1r, a1s, a1r,
    b2s, b2r, a2s, a2r, a3s, a3r, b3s, b3r,
    h0s, h0r, h1s, h1r,
    kxs, kxr, kls, klr, fgs, fgr, bgs, bgr,
    ssem, rsem,
):
    seq = lax.axis_index("seq")
    chan = lax.axis_index("chan")
    mx = lax.rem(seq, NX)
    ml = lax.div(seq, NX)
    ahead = lax.rem(seq + 1, SEQ)
    behind = lax.rem(seq + SEQ - 1, SEQ)

    def x_peer(d):
        other = lax.rem(mx + d, NX)
        return other, (ml * NX + other, chan)

    def l_peer(d):
        other = lax.rem(ml + d, NL)
        return other, (other * NX + mx, chan)

    def c_peer(d):
        other = lax.rem(chan + d, CHAN)
        return other, (seq, other)

    barrier = pltpu.get_barrier_semaphore()

    def greet(peer, count):
        def step(d, carry):
            pl.semaphore_signal(barrier, inc=1, device_id=peer(d)[1], device_id_type=MESH)
            return carry

        lax.fori_loop(1, count, step, 0)

    greet(x_peer, NX)
    greet(l_peer, NL)
    greet(c_peer, CHAN)
    pl.semaphore_signal(barrier, inc=1, device_id=(ahead, chan), device_id_type=MESH)
    pl.semaphore_signal(barrier, inc=1, device_id=(behind, chan), device_id_type=MESH)

    def scatter(send, recv, mine, peer, count, sem):
        def step(d, carry):
            other, device = peer(d)
            pltpu.make_async_remote_copy(
                src_ref=send.at[other], dst_ref=recv.at[mine],
                send_sem=ssem.at[sem], recv_sem=rsem.at[sem],
                device_id=device, device_id_type=MESH,
            ).start()
            return carry

        lax.fori_loop(1, count, step, 0)
        recv[mine] = send[mine]

    def arrive(recv, count, sem):
        part = recv.at[pl.ds(0, count - 1)]
        pltpu.make_async_copy(part, part, rsem.at[sem]).wait()

    def sent(send, count, sem):
        part = send.at[pl.ds(0, count - 1)]
        pltpu.make_async_copy(part, part, ssem.at[sem]).wait()

    def spread(send, recv, mine, peer, count, sem):
        def step(d, carry):
            other, device = peer(d)
            pltpu.make_async_remote_copy(
                src_ref=send, dst_ref=recv.at[mine],
                send_sem=ssem.at[sem], recv_sem=rsem.at[sem],
                device_id=device, device_id_type=MESH,
            ).start()
            return carry

        lax.fori_loop(1, count, step, 0)
        recv[mine] = send[...]

    def hand(send, recv, device, sem):
        copy = pltpu.make_async_remote_copy(
            src_ref=send, dst_ref=recv, send_sem=ssem.at[sem], recv_sem=rsem.at[sem],
            device_id=(device, chan), device_id_type=MESH,
        )
        copy.start()
        return copy

    def flat(ref):
        return ref[...].reshape(256, LANES)

    zero_rows = jnp.zeros((LANES - ROWS, EXT), BF)
    xs[0:ROWS, :] = x_ref[...].reshape(ROWS, EXT)
    xs[ROWS:LANES, :] = zero_rows
    cs[0:ROWS, :] = c_ref[...].reshape(ROWS, EXT)
    cs[ROWS:LANES, :] = zero_rows

    h0s[...] = nt(hot((16, EXT), lambda r, c: (r == c) & (r < 2)), cs[...]).astype(BF)
    m0 = nn(xs[:, 0:BLK], f_ref[0]).astype(BF)
    m1 = nn(xs[:, BLK:EXT], f_ref[1]).astype(BF)
    p0 = hot((256, 256), place0)
    a0s[...] = (nt(p0[:, 0:BLK], m0) + nt(p0[:, BLK:EXT], m1)).astype(BF).reshape(NX, 32, LANES)

    pl.semaphore_wait(barrier, NX - 1 + NL - 1 + CHAN - 1 + 2)

    halo0 = hand(h0s, h0r, behind, 16)
    scatter(a0s, a0r, mx, x_peer, NX, 0)

    kpad[...] = jnp.zeros_like(kpad)
    kpad[0:3, 0:CH] = k_ref[...]
    taps = jnp.concatenate([kpad[:, 0:128].T, kpad[:, 128:256].T], axis=0)
    kcol[0:CH, :] = taps[0:CH]
    kcol[CH:ROWS, :] = taps[0:CH]
    kcol[ROWS:LANES, :] = jnp.zeros((LANES - ROWS, 128), F32)

    cot = cs[...]
    near1 = nn(cot, hot((EXT, EXT), lambda r, c: r == c + 1))
    near2 = nn(cot, hot((EXT, EXT), lambda r, c: r == c + 2))
    halo0.wait_recv()
    keep = (seq < SEQ - 1).astype(F32)
    tail = (h0r[...].astype(F32) * keep).astype(BF)
    near1 = near1 + tn(tail, hot((16, EXT), lambda r, c: (r == 0) & (c == EXT - 1)))
    near2 = near2 + tn(tail, hot((16, EXT), lambda r, c: (r < 2) & (c == EXT - 2 + r)))
    prod_w[0] = near1.astype(BF)
    prod_w[1] = near2.astype(BF)
    gate[...] = kcol[:, 0:1] * cot.astype(F32) + kcol[:, 1:2] * near1 + kcol[:, 2:3] * near2
    mgrad = (gate[...] * xs[...].astype(F32)).astype(BF)
    b1s[...] = nt(hot((256, 256), place1), mgrad).astype(BF).reshape(NL, 16, LANES)
    scatter(b1s, b1r, ml, l_peer, NL, 1)

    eye = hot((256, 256), lambda r, c: r == c)
    second = s_ref[0]
    st[...] = nt(eye, second).astype(BF)
    back = hot((256, 256), flip(order1))
    s11[...] = nt(nn(back, second).astype(BF), back).astype(BF)
    xt[...] = nt(eye, xs[...]).astype(BF)

    arrive(a0r, NX, 0)
    b0s[...] = nn(hot((256, 256), turn0), flat(a0r)).astype(BF).reshape(NL, 16, LANES)
    scatter(b0s, b0r, ml, l_peer, NL, 2)

    arrive(b1r, NL, 1)
    a1s[...] = nn(hot((256, 256), turn1), flat(b1r)).astype(BF).reshape(NX, 32, LANES)
    scatter(a1s, a1r, mx, x_peer, NX, 3)

    arrive(b0r, NL, 2)
    b2s[...] = nn(st[...], flat(b0r)).astype(BF).reshape(NL, 16, LANES)
    scatter(b2s, b2r, ml, l_peer, NL, 4)

    arrive(a1r, NX, 3)
    a3s[...] = nn(s11[...], flat(a1r)).astype(BF).reshape(NX, 32, LANES)
    scatter(a3s, a3r, mx, x_peer, NX, 5)

    mg_nat = nn(hot((256, 256), order1), flat(a1r)).astype(BF)
    fgs[...] = nt(flat(b0r), mg_nat).reshape(CHAN, 64, 256)
    scatter(fgs, fgr, chan, c_peer, CHAN, 6)

    arrive(b2r, NL, 4)
    a2s[...] = nn(hot((256, 256), flip(turn0)), flat(b2r)).astype(BF).reshape(NX, 32, LANES)
    scatter(a2s, a2r, mx, x_peer, NX, 7)

    arrive(a3r, NX, 5)
    b3s[...] = nn(hot((256, 256), flip(turn1)), flat(a3r)).astype(BF).reshape(NL, 16, LANES)
    scatter(b3s, b3r, ml, l_peer, NL, 8)

    arrive(a2r, NX, 7)
    monarch = tn(flat(a2r), hot((256, 256), place0))
    gated = (xs[...].astype(F32) * monarch).astype(BF)
    h1s[...] = nt(hot((16, EXT), lambda r, c: (r < 2) & (c == EXT - 2 + r)), gated).astype(BF)
    halo1 = hand(h1s, h1r, ahead, 17)
    gate[...] = gate[...] * monarch

    gated32 = gated.astype(F32)
    kg = jnp.zeros((8, CH), F32)
    for j in range(3):
        pick = hot((8, EXT), lambda r, c: (r == j) & (c >= 0))
        window = cs[...] if j == 0 else prod_w[j - 1]
        prod = gated32 * window.astype(F32)
        high = prod.astype(BF)
        low = (prod - high.astype(F32)).astype(BF)
        for b in range(BATCH):
            rows = slice(b * CH, (b + 1) * CH)
            kg = kg + nt(pick, high[rows]) + nt(pick, low[rows])
    kxs[...] = jnp.zeros_like(kxs)
    kxs[:, 0:CH] = kg
    spread(kxs, kxr, mx, x_peer, NX, 9)

    far1 = nn(gated, hot((EXT, EXT), lambda r, c: r + 1 == c))
    far2 = nn(gated, hot((EXT, EXT), lambda r, c: r + 2 == c))
    total = kcol[:, 0:1] * gated32 + kcol[:, 1:2] * far1 + kcol[:, 2:3] * far2

    arrive(b3r, NL, 8)
    mgr[...] = tn(flat(b3r), hot((256, 256), place1)).astype(BF)
    for q in range(2):
        lanes = slice(q * BLK, (q + 1) * BLK)
        part = nn(xt[lanes, :], mgr[:, lanes]).reshape(CHAN, 32, BLK)
        for o in range(CHAN):
            bgs[o, q] = part[o]
    scatter(bgs, bgr, chan, c_peer, CHAN, 10)

    arrive(kxr, NX, 9)
    kls[...] = sum((kxr[i] for i in range(1, NX)), kxr[0])
    spread(kls, klr, ml, l_peer, NL, 11)

    for q in range(2):
        lanes = slice(q * BLK, (q + 1) * BLK)
        through = nt(mgr[:, lanes], f_ref[q])
        out = (gate[:, lanes] + through)[0:ROWS].astype(BF)
        igrad_ref[:, :, lanes] = out.reshape(BATCH, CH, BLK)

    halo1.wait_recv()
    keep = (seq > 0).astype(F32)
    prior = (h1r[...].astype(F32) * keep).astype(BF)
    edge1 = tn(prior, hot((16, EXT), lambda r, c: (r == 1) & (c == 0)))
    edge2 = tn(prior, hot((16, EXT), lambda r, c: (r < 2) & (r == c)))
    total = total + (kcol[:, 1:2] * edge1 + kcol[:, 2:3] * edge2)
    mixed_ref[...] = total[0:ROWS].astype(BF).reshape(BATCH, CH, EXT)

    arrive(fgr, CHAN, 6)
    fgrad_ref[0] = (fgr[0] + fgr[1]) + (fgr[2] + fgr[3])
    arrive(bgr, CHAN, 10)
    bgrad_ref[...] = (bgr[0] + bgr[1]) + (bgr[2] + bgr[3])
    arrive(klr, NL, 11)
    whole = sum((klr[i] for i in range(1, NL)), klr[0])
    kgrad_ref[...] = whole[0:3, 0:CH]

    halo0.wait_send()
    halo1.wait_send()
    sent(a0s, NX, 0)
    sent(b1s, NL, 1)
    sent(b0s, NL, 2)
    sent(a1s, NX, 3)
    sent(b2s, NL, 4)
    sent(a3s, NX, 5)
    sent(fgs, CHAN, 6)
    sent(a2s, NX, 7)
    sent(b3s, NL, 8)
    sent(kxr, NX, 9)
    sent(bgs, CHAN, 10)
    sent(klr, NL, 11)


def shards(inputs, first_blocks, second_blocks, kernel, cotangent):
    vmem = pl.BlockSpec(memory_space=pltpu.VMEM)
    xbuf = pltpu.VMEM((NX, 32, LANES), BF)
    lbuf = pltpu.VMEM((NL, 16, LANES), BF)
    halo = pltpu.VMEM((16, LANES), BF)
    return pl.pallas_call(
        body,
        out_shape=(
            jax.ShapeDtypeStruct((BATCH, CH, EXT), BF),
            jax.ShapeDtypeStruct((BATCH, CH, EXT), BF),
            jax.ShapeDtypeStruct((3, CH), F32),
            jax.ShapeDtypeStruct((2, BLK // CHAN, BLK), F32),
            jax.ShapeDtypeStruct((1, 256 // CHAN, 256), F32),
        ),
        in_specs=[vmem] * 5,
        out_specs=(vmem,) * 5,
        scratch_shapes=[
            pltpu.VMEM((LANES, EXT), BF),
            pltpu.VMEM((LANES, EXT), BF),
            pltpu.VMEM((EXT, LANES), BF),
            pltpu.VMEM((LANES, EXT), F32),
            pltpu.VMEM((128, 256), F32),
            pltpu.VMEM((LANES, 128), F32),
            pltpu.VMEM((2, LANES, EXT), BF),
            pltpu.VMEM((256, 256), BF),
            pltpu.VMEM((256, 256), BF),
            pltpu.VMEM((LANES, EXT), BF),
            xbuf, xbuf, lbuf, lbuf, lbuf, lbuf, xbuf, xbuf,
            lbuf, lbuf, xbuf, xbuf, xbuf, xbuf, lbuf, lbuf,
            halo, halo, halo, halo,
            pltpu.VMEM((8, 256), F32), pltpu.VMEM((NX, 8, 256), F32),
            pltpu.VMEM((8, 256), F32), pltpu.VMEM((NL, 8, 256), F32),
            pltpu.VMEM((CHAN, 64, 256), F32), pltpu.VMEM((CHAN, 64, 256), F32),
            pltpu.VMEM((CHAN, 2, 32, BLK), F32), pltpu.VMEM((CHAN, 2, 32, BLK), F32),
            pltpu.SemaphoreType.DMA((18,)),
            pltpu.SemaphoreType.DMA((18,)),
        ],
        compiler_params=pltpu.CompilerParams(
            collective_id=0, has_side_effects=True, vmem_limit_bytes=40 * 1024 * 1024
        ),
    )(inputs, first_blocks, second_blocks, kernel, cotangent)


def solution(mesh):
    placed = (
        P(None, "chan", "seq"),
        P("seq", None, None),
        P("seq", None, None),
        P(None, "chan"),
        P(None, "chan", "seq"),
    )
    return jax.shard_map(
        shards,
        mesh=mesh,
        in_specs=placed,
        out_specs=(
            P(None, "chan", "seq"),
            P(None, "chan", "seq"),
            P(None, "chan"),
            P("seq", "chan", None),
            P("seq", "chan", None),
        ),
        check_vma=False,
    )
```

```python
import jax
import jax.numpy as jnp
from jax import lax
from jax.experimental import pallas as pl
from jax.experimental.pallas import tpu as pltpu
from jax.sharding import PartitionSpec as P

NX, NL = 8, 16
SEQ, CHAN = NX * NL, 4
BATCH, CH, EXT, BLK = 2, 240, 256, 128
ROWS = 256
MESH = pl.DeviceIdType.MESH
BF, F32 = jnp.bfloat16, jnp.float32
A0, B0, B1, A1, B2, A2, A3, B3 = range(0, 16, 2)
FG, BG, KX, KL, H0, H1 = range(16, 22)


def dot(a, b, ca, cb):
    return lax.dot_general(a, b, (((ca,), (cb,)), ((), ())), preferred_element_type=F32)


def nn(a, b):
    return dot(a, b, 1, 0)


def nt(a, b):
    return dot(a, b, 1, 1)


def tn(a, b):
    return dot(a, b, 0, 0)


def hot(shape, where):
    row = lax.broadcasted_iota(jnp.int32, shape, 0)
    col = lax.broadcasted_iota(jnp.int32, shape, 1)
    return jnp.where(where(row, col), 1.0, 0.0).astype(BF)


def place0(r, c):
    return ((r >> 4) & 1) * 128 + (r & 15) * 8 + (r >> 5) == c


def turn0(r, c):
    return ((r >> 1) & 7) * 32 + (r & 1) * 16 + (r >> 4) == c


def place1(r, c):
    return ((r >> 3) & 1) * 128 + (r >> 4) * 8 + (r & 7) == c


def turn1(r, c):
    return ((r >> 1) & 15) * 16 + (r & 1) * 8 + (r >> 5) == c


def order1(r, c):
    return ((r >> 1) & 7) * 32 + (r >> 4) * 2 + (r & 1) == c


def flip(where):
    return lambda r, c: where(c, r)


def body(
    x_in, f_in, s_in, k_in, c_in,
    mixed_ref, igrad_ref, kgrad_ref, bgrad_ref, fgrad_ref,
    xs, cs, fs, sec, kin, xt, gate, total, gat, mgrad, near, kpad, kcol, st, s11, mgr, tables,
    a0s, a0r, b0s, b0r, b1s, b1r, a1s, a1r,
    b2s, b2r, a2s, a2r, a3s, a3r, b3s, b3r,
    h0s, h0r, h1s, h1r,
    kxs, kxr, kls, klr, fgo, fgs, fgr, bgo, bgs, bgr,
    ssem, rsem, isem,
):
    seq = lax.axis_index("seq")
    chan = lax.axis_index("chan")
    mx = lax.rem(seq, NX)
    ml = lax.div(seq, NX)
    ahead = lax.rem(seq + 1, SEQ)
    behind = lax.rem(seq + SEQ - 1, SEQ)

    def x_peer(d):
        other = lax.rem(mx + d, NX)
        return other, (ml * NX + other, chan)

    def l_peer(d):
        other = lax.rem(ml + d, NL)
        return other, (other * NX + mx, chan)

    def c_peer(d):
        other = lax.rem(chan + d, CHAN)
        return other, (seq, other)

    barrier = pltpu.get_barrier_semaphore()

    def greet(peer, count):
        def step(d, carry):
            pl.semaphore_signal(barrier, inc=1, device_id=peer(d)[1], device_id_type=MESH)
            return carry

        lax.fori_loop(1, count, step, 0)

    loads = [
        pltpu.make_async_copy(x_in, xs.at[:, pl.ds(0, CH), :], isem.at[0]),
        pltpu.make_async_copy(f_in, fs, isem.at[1]),
        pltpu.make_async_copy(c_in, cs.at[:, pl.ds(0, CH), :], isem.at[2]),
        pltpu.make_async_copy(k_in, kin, isem.at[3]),
        pltpu.make_async_copy(s_in, sec, isem.at[4]),
    ]
    for load in loads:
        load.start()
    greet(x_peer, NX)
    greet(l_peer, NL)
    greet(c_peer, CHAN)
    pl.semaphore_signal(barrier, inc=1, device_id=(ahead, chan), device_id_type=MESH)
    pl.semaphore_signal(barrier, inc=1, device_id=(behind, chan), device_id_type=MESH)

    def remote(src, dst, device, sem):
        return pltpu.make_async_remote_copy(
            src_ref=src, dst_ref=dst, send_sem=ssem.at[sem], recv_sem=rsem.at[sem],
            device_id=device, device_id_type=MESH,
        )

    def scatter(send, recv, mine, peer, count, sem):
        def step(i, carry):
            d = count // 2 + lax.div(i + 1, 2) * (2 * lax.rem(i, 2) - 1)
            other, device = peer(d)
            remote(send.at[other], recv.at[mine], device, sem).start()
            return carry

        lax.fori_loop(0, count - 1, step, 0)

    def keep(send, recv, mine):
        recv[mine] = send[mine]

    def spread(send, recv, mine, peer, count, sem):
        def step(i, carry):
            d = count // 2 + lax.div(i + 1, 2) * (2 * lax.rem(i, 2) - 1)
            remote(send, recv.at[mine], peer(d)[1], sem).start()
            return carry

        lax.fori_loop(0, count - 1, step, 0)
        recv[mine] = send[...]

    def arrive(recv, count, sem):
        part = recv.at[pl.ds(0, count - 1)]
        pltpu.make_async_copy(part, part, rsem.at[sem]).wait()

    def sent(send, count, sem):
        part = send.at[pl.ds(0, count - 1)]
        pltpu.make_async_copy(part, part, ssem.at[sem]).wait()

    def flat(ref, b):
        return ref[b].reshape(256, ROWS)

    def over_x(value, send, recv, b, sem):
        send[b] = value.astype(BF).reshape(NX, 32, ROWS)
        scatter(send.at[b], recv.at[b], mx, x_peer, NX, sem + b)
        keep(send.at[b], recv.at[b], mx)

    def over_l(value, send, recv, b, sem):
        send[b] = value.astype(BF).reshape(NL, 16, ROWS)
        scatter(send.at[b], recv.at[b], ml, l_peer, NL, sem + b)
        keep(send.at[b], recv.at[b], ml)

    zero_rows = jnp.zeros((BATCH, ROWS - CH, EXT), BF)
    xs[:, CH:ROWS, :] = zero_rows
    cs[:, CH:ROWS, :] = zero_rows
    kpad[...] = jnp.zeros_like(kpad)
    tables[0] = hot((256, 256), place0)
    tables[1] = hot((256, 256), place1)
    shift1 = hot((EXT, EXT), lambda r, c: r == c + 1)
    shift2 = hot((EXT, EXT), lambda r, c: r == c + 2)

    loads[0].wait()
    loads[1].wait()
    p0 = tables[0]
    for b in range(BATCH):
        m0 = nn(xs[b, :, 0:BLK], fs[0]).astype(BF)
        m1 = nn(xs[b, :, BLK:EXT], fs[1]).astype(BF)
        a0s[b] = (nt(p0[:, 0:BLK], m0) + nt(p0[:, BLK:EXT], m1)).astype(BF).reshape(NX, 32, ROWS)
    loads[2].wait()
    head = hot((16, EXT), lambda r, c: (r == c) & (r < 2))
    for b in range(BATCH):
        h0s[b] = nt(head, cs[b]).astype(BF)

    pl.semaphore_wait(barrier, NX - 1 + NL - 1 + CHAN - 1 + 2)

    halo0 = remote(h0s, h0r, (behind, chan), H0)
    halo0.start()
    for b in range(BATCH):
        scatter(a0s.at[b], a0r.at[b], mx, x_peer, NX, A0 + b)
        keep(a0s.at[b], a0r.at[b], mx)

    loads[3].wait()
    kpad[0:3, 0:CH] = kin[...]
    kcol[0:128, :] = kpad[:, 0:128].T
    kcol[128:256, :] = kpad[:, 128:256].T

    def gate_from(lanes, b, cot, near1, near2):
        near[0, b, :, lanes] = near1.astype(BF)
        near[1, b, :, lanes] = near2.astype(BF)
        value = kcol[:, 0:1] * cot.astype(F32) + kcol[:, 1:2] * near1 + kcol[:, 2:3] * near2
        gate[b, :, lanes] = value
        mgrad[b, :, lanes] = (value * xs[b, :, lanes].astype(F32)).astype(BF)

    last = NL - 1
    p1 = tables[1]
    for b in range(BATCH):
        gate_from(slice(0, EXT), b, cs[b], nn(cs[b], shift1), nn(cs[b], shift2))
        b1s[b] = nt(p1, mgrad[b]).astype(BF).reshape(NL, 16, ROWS)

        def step(i, carry):
            other, device = l_peer(NL // 2 + lax.div(i + 1, 2) * (2 * lax.rem(i, 2) - 1))

            @pl.when(other != last)
            def _():
                remote(b1s.at[b, other], b1r.at[b, ml], device, B1 + b).start()

            return carry

        lax.fori_loop(0, NL - 1, step, 0)

    halo0.wait_recv()
    inside = (seq < SEQ - 1).astype(F32)
    high = slice(BLK, EXT)
    for b in range(BATCH):
        tail = (h0r[b].astype(F32) * inside).astype(BF)
        near1 = near[0, b, :, high].astype(F32)
        near2 = near[1, b, :, high].astype(F32)
        near1 = near1 + tn(tail, hot((16, BLK), lambda r, c: (r == 0) & (c == BLK - 1)))
        near2 = near2 + tn(tail, hot((16, BLK), lambda r, c: (r < 2) & (c == BLK - 2 + r)))
        gate_from(high, b, cs[b, :, high], near1, near2)
        b1s[b, last] = nt(tables[1, 16 * last : 16 * NL], mgrad[b]).astype(BF)

        @pl.when(ml != last)
        def _():
            remote(b1s.at[b, last], b1r.at[b, ml], (last * NX + mx, chan), B1 + b).start()

        keep(b1s.at[b], b1r.at[b], ml)

    tables[2] = hot((256, 256), turn0)
    tables[3] = hot((256, 256), flip(turn0))
    tables[4] = hot((256, 256), turn1)
    tables[5] = hot((256, 256), flip(turn1))
    tables[6] = hot((256, 256), order1)
    loads[4].wait()
    eye = hot((256, 256), lambda r, c: r == c)
    second = sec[0]
    st[...] = nt(eye, second).astype(BF)
    back = hot((256, 256), flip(order1))
    s11[...] = nt(nn(back, second).astype(BF), back).astype(BF)

    for b in range(BATCH):
        arrive(a0r.at[b], NX, A0 + b)
        over_l(nn(tables[2], flat(a0r, b)), b0s, b0r, b, B0)
    for b in range(BATCH):
        arrive(b1r.at[b], NL, B1 + b)
        over_x(nn(tables[4], flat(b1r, b)), a1s, a1r, b, A1)
    for b in range(BATCH):
        arrive(a1r.at[b], NX, A1 + b)
        over_x(nn(s11[...], flat(a1r, b)), a3s, a3r, b, A3)
        arrive(b0r.at[b], NL, B0 + b)
        over_l(nn(st[...], flat(b0r, b)), b2s, b2r, b, B2)
    for b in range(BATCH):
        arrive(a3r.at[b], NX, A3 + b)
        over_l(nn(tables[5], flat(a3r, b)), b3s, b3r, b, B3)
    grad = jnp.zeros((256, 256), F32)
    for b in range(BATCH):
        nat = nn(tables[6], flat(a1r, b)).astype(BF)
        grad = grad + nt(flat(b0r, b), nat)
    fgo[...] = grad.reshape(CHAN, 64, 256)
    fgs[...] = grad.astype(BF).reshape(CHAN, 64, 256)
    scatter(fgs, fgr, chan, c_peer, CHAN, FG)
    for b in range(BATCH):
        xt[b] = nt(eye, xs[b]).astype(BF)
    for b in range(BATCH):
        arrive(b2r.at[b], NL, B2 + b)
        over_x(nn(tables[3], flat(b2r, b)), a2s, a2r, b, A2)

    edge = hot((16, EXT), lambda r, c: (r < 2) & (c == EXT - 2 + r))
    prods = [jnp.zeros((ROWS, BLK), F32)] * 3
    for b in range(BATCH):
        arrive(a2r.at[b], NX, A2 + b)
        monarch = tn(flat(a2r, b), tables[0])
        gated = (xs[b].astype(F32) * monarch).astype(BF)
        gat[b] = gated
        h1s[b] = nt(edge, gated).astype(BF)
        gate[b] = gate[b] * monarch
        gated32 = gated.astype(F32)
        for j in range(3):
            window = cs[b] if j == 0 else near[j - 1, b]
            prod = gated32 * window.astype(F32)
            prods[j] = prods[j] + (prod[:, 0:BLK] + prod[:, BLK:EXT])
    halo1 = remote(h1s, h1r, (ahead, chan), H1)
    halo1.start()
    sums = [jnp.sum(prod, axis=1, keepdims=True) for prod in prods]
    lane = lax.broadcasted_iota(jnp.int32, (ROWS, 128), 1)
    wide = jnp.where(lane == 0, sums[0], jnp.where(lane == 1, sums[1], sums[2]))
    kxs[:, 0:128] = wide[0:128].T[0:8]
    kxs[:, 128:256] = wide[128:256].T[0:8]
    spread(kxs, kxr, mx, x_peer, NX, KX)

    far1 = hot((EXT, EXT), lambda r, c: r + 1 == c)
    far2 = hot((EXT, EXT), lambda r, c: r + 2 == c)
    for b in range(BATCH):
        total[b] = (
            kcol[:, 0:1] * gat[b].astype(F32)
            + kcol[:, 1:2] * nn(gat[b], far1)
            + kcol[:, 2:3] * nn(gat[b], far2)
        )

    for b in range(BATCH):
        arrive(b3r.at[b], NL, B3 + b)
        mgr[b] = tn(flat(b3r, b), tables[1]).astype(BF)
    for q in range(2):
        lanes = slice(q * BLK, (q + 1) * BLK)
        part = nn(xt[0, lanes, :], mgr[0, :, lanes]) + nn(xt[1, lanes, :], mgr[1, :, lanes])
        part = part.reshape(CHAN, 32, BLK)
        for o in range(CHAN):
            bgo[o, q] = part[o]
            bgs[o, q] = part[o].astype(BF)
    scatter(bgs, bgr, chan, c_peer, CHAN, BG)

    arrive(kxr, NX, KX)
    kls[...] = sum((kxr[i] for i in range(1, NX)), kxr[0])
    spread(kls, klr, ml, l_peer, NL, KL)

    for q in range(2):
        lanes = slice(q * BLK, (q + 1) * BLK)
        for b in range(BATCH):
            through = nt(mgr[b, :, lanes], fs[q])
            igrad_ref[b, :, lanes] = (gate[b, :, lanes] + through)[0:CH].astype(BF)

    halo1.wait_recv()
    inside = (seq > 0).astype(F32)
    mixed_ref[:, :, high] = total[:, 0:CH, high].astype(BF)
    for b in range(BATCH):
        prior = (h1r[b].astype(F32) * inside).astype(BF)
        edge1 = tn(prior, hot((16, BLK), lambda r, c: (r == 1) & (c == 0)))
        edge2 = tn(prior, hot((16, BLK), lambda r, c: (r < 2) & (r == c)))
        value = total[b, :, 0:BLK] + (kcol[:, 1:2] * edge1 + kcol[:, 2:3] * edge2)
        mixed_ref[b, :, 0:BLK] = value[0:CH].astype(BF)

    arrive(fgr, CHAN, FG)
    fgr[chan] = jnp.zeros((64, 256), BF)
    got = [fgr[i].astype(F32) for i in range(CHAN)]
    fgrad_ref[0] = fgo[chan] + ((got[0] + got[1]) + (got[2] + got[3]))
    arrive(bgr, CHAN, BG)
    bgr[chan] = jnp.zeros((2, 32, BLK), BF)
    got = [bgr[i].astype(F32) for i in range(CHAN)]
    bgrad_ref[...] = bgo[chan] + ((got[0] + got[1]) + (got[2] + got[3]))
    arrive(klr, NL, KL)
    whole = sum((klr[i] for i in range(1, NL)), klr[0])
    kgrad_ref[...] = whole[0:3, 0:CH]

    halo0.wait_send()
    halo1.wait_send()
    for b in range(BATCH):
        for send, sem in ((a0s, A0), (a1s, A1), (a2s, A2), (a3s, A3)):
            sent(send.at[b], NX, sem + b)
        for send, sem in ((b0s, B0), (b1s, B1), (b2s, B2), (b3s, B3)):
            sent(send.at[b], NL, sem + b)
    sent(fgs, CHAN, FG)
    sent(bgs, CHAN, BG)
    sent(kxr, NX, KX)
    sent(klr, NL, KL)


def emit(*refs):
    count = (len(refs) - 1) // 2
    sem = refs[-1]
    copies = [pltpu.make_async_copy(refs[i], refs[count + i], sem.at[i]) for i in range(count)]
    for copy in copies:
        copy.start()
    for copy in copies:
        copy.wait()


def shards(inputs, first_blocks, second_blocks, kernel, cotangent):
    vmem = pl.BlockSpec(memory_space=pltpu.VMEM)
    free = pl.BlockSpec(memory_space=pl.ANY)
    xbuf = pltpu.VMEM((BATCH, NX, 32, ROWS), BF)
    lbuf = pltpu.VMEM((BATCH, NL, 16, ROWS), BF)
    halo = pltpu.VMEM((BATCH, 16, ROWS), BF)
    plane = pltpu.VMEM((BATCH, ROWS, EXT), BF)
    square = pltpu.VMEM((256, 256), BF)
    shapes = (
        jax.ShapeDtypeStruct((BATCH, CH, EXT), BF),
        jax.ShapeDtypeStruct((BATCH, CH, EXT), BF),
        jax.ShapeDtypeStruct((3, CH), F32),
        jax.ShapeDtypeStruct((2, BLK // CHAN, BLK), F32),
        jax.ShapeDtypeStruct((1, 256 // CHAN, 256), F32),
    )
    results = pl.pallas_call(
        body,
        out_shape=shapes,
        in_specs=[free] * 5,
        out_specs=(vmem,) * 5,
        scratch_shapes=[
            plane, plane,
            pltpu.VMEM((2, BLK, BLK), BF), pltpu.VMEM((1, 256, 256), BF),
            pltpu.VMEM((3, CH), F32), plane,
            pltpu.VMEM((BATCH, ROWS, EXT), F32), pltpu.VMEM((BATCH, ROWS, EXT), F32),
            plane, plane,
            pltpu.VMEM((2, BATCH, ROWS, EXT), BF),
            pltpu.VMEM((128, 256), F32), pltpu.VMEM((ROWS, 128), F32),
            square, square, plane,
            pltpu.VMEM((7, 256, 256), BF),
            xbuf, xbuf, lbuf, lbuf, lbuf, lbuf, xbuf, xbuf,
            lbuf, lbuf, xbuf, xbuf, xbuf, xbuf, lbuf, lbuf,
            halo, halo, halo, halo,
            pltpu.VMEM((8, 256), F32), pltpu.VMEM((NX, 8, 256), F32),
            pltpu.VMEM((8, 256), F32), pltpu.VMEM((NL, 8, 256), F32),
            pltpu.VMEM((CHAN, 64, 256), F32),
            pltpu.VMEM((CHAN, 64, 256), BF), pltpu.VMEM((CHAN, 64, 256), BF),
            pltpu.VMEM((CHAN, 2, 32, BLK), F32),
            pltpu.VMEM((CHAN, 2, 32, BLK), BF), pltpu.VMEM((CHAN, 2, 32, BLK), BF),
            pltpu.SemaphoreType.DMA((22,)),
            pltpu.SemaphoreType.DMA((22,)),
            pltpu.SemaphoreType.DMA((5,)),
        ],
        compiler_params=pltpu.CompilerParams(
            collective_id=0, has_side_effects=True, vmem_limit_bytes=60 * 1024 * 1024
        ),
    )(inputs, first_blocks, second_blocks, kernel, cotangent)
    return pl.pallas_call(
        emit,
        out_shape=shapes,
        in_specs=[free] * 5,
        out_specs=(free,) * 5,
        scratch_shapes=[pltpu.SemaphoreType.DMA((5,))],
        compiler_params=pltpu.CompilerParams(vmem_limit_bytes=60 * 1024 * 1024),
    )(*results)


def solution(mesh):
    placed = (
        P(None, "chan", "seq"),
        P("seq", None, None),
        P("seq", None, None),
        P(None, "chan"),
        P(None, "chan", "seq"),
    )
    return jax.shard_map(
        shards,
        mesh=mesh,
        in_specs=placed,
        out_specs=(
            P(None, "chan", "seq"),
            P(None, "chan", "seq"),
            P(None, "chan"),
            P("seq", "chan", None),
            P("seq", "chan", None),
        ),
        check_vma=False,
    )
```

```python
import jax
import jax.numpy as jnp
from jax import lax
from jax.experimental import pallas as pl
from jax.experimental.pallas import tpu as pltpu
from jax.sharding import PartitionSpec as P

NX, NL = 8, 16
SEQ, CHAN = NX * NL, 4
BATCH, CH, EXT, BLK = 2, 240, 256, 128
ROWS = 256
MESH = pl.DeviceIdType.MESH
BF, F32 = jnp.bfloat16, jnp.float32
A0, B0, B1, A1, B2, A2, A3, B3 = range(0, 16, 2)
FG, BG, KX, KL, H0, H1 = range(16, 22)


def dot(a, b, ca, cb):
    return lax.dot_general(a, b, (((ca,), (cb,)), ((), ())), preferred_element_type=F32)


def nn(a, b):
    return dot(a, b, 1, 0)


def nt(a, b):
    return dot(a, b, 1, 1)


def tn(a, b):
    return dot(a, b, 0, 0)


def hot(shape, where):
    row = lax.broadcasted_iota(jnp.int32, shape, 0)
    col = lax.broadcasted_iota(jnp.int32, shape, 1)
    return jnp.where(where(row, col), 1.0, 0.0).astype(BF)


def place0(r, c):
    return ((r >> 4) & 1) * 128 + (r & 15) * 8 + (r >> 5) == c


def turn0(r, c):
    return ((r >> 1) & 7) * 32 + (r & 1) * 16 + (r >> 4) == c


def place1(r, c):
    return ((r >> 3) & 1) * 128 + (r >> 4) * 8 + (r & 7) == c


def turn1(r, c):
    return ((r >> 1) & 15) * 16 + (r & 1) * 8 + (r >> 5) == c


def order1(r, c):
    return ((r >> 1) & 7) * 32 + (r >> 4) * 2 + (r & 1) == c


def flip(where):
    return lambda r, c: where(c, r)


def body(
    x_in, f_in, s_in, k_in, c_in,
    mixed_ref, igrad_ref, kgrad_ref, bgrad_ref, fgrad_ref,
    xs, cs, fs, sec, kin, xt, gate, total, gat, mgrad, near, kpad, kcol, st, s11, mgr, tables,
    a0s, a0r, b0s, b0r, b1s, b1r, a1s, a1r,
    b2s, b2r, a2s, a2r, a3s, a3r, b3s, b3r,
    h0s, h0r, h1s, h1r,
    kxs, kxr, kls, klr, fgo, fgs, fgr, bgo, bgs, bgr,
    ssem, rsem, isem,
):
    seq = lax.axis_index("seq")
    chan = lax.axis_index("chan")
    mx = lax.rem(seq, NX)
    ml = lax.div(seq, NX)
    ahead = lax.rem(seq + 1, SEQ)
    behind = lax.rem(seq + SEQ - 1, SEQ)

    def x_peer(d):
        other = lax.rem(mx + d, NX)
        return other, (ml * NX + other, chan)

    def l_peer(d):
        other = lax.rem(ml + d, NL)
        return other, (other * NX + mx, chan)

    def c_peer(d):
        other = lax.rem(chan + d, CHAN)
        return other, (seq, other)

    barrier = pltpu.get_barrier_semaphore()

    def greet(peer, count):
        def step(d, carry):
            pl.semaphore_signal(barrier, inc=1, device_id=peer(d)[1], device_id_type=MESH)
            return carry

        lax.fori_loop(1, count, step, 0)

    loads = [
        pltpu.make_async_copy(x_in, xs.at[:, pl.ds(0, CH), :], isem.at[0]),
        pltpu.make_async_copy(f_in, fs, isem.at[1]),
        pltpu.make_async_copy(c_in, cs.at[:, pl.ds(0, CH), :], isem.at[2]),
        pltpu.make_async_copy(k_in, kin, isem.at[3]),
        pltpu.make_async_copy(s_in, sec, isem.at[4]),
    ]
    for load in loads:
        load.start()
    greet(x_peer, NX)
    greet(l_peer, NL)
    greet(c_peer, CHAN)
    pl.semaphore_signal(barrier, inc=1, device_id=(ahead, chan), device_id_type=MESH)
    pl.semaphore_signal(barrier, inc=1, device_id=(behind, chan), device_id_type=MESH)

    def remote(src, dst, device, sem):
        return pltpu.make_async_remote_copy(
            src_ref=src, dst_ref=dst, send_sem=ssem.at[sem], recv_sem=rsem.at[sem],
            device_id=device, device_id_type=MESH,
        )

    def scatter(send, recv, mine, peer, count, sem):
        def step(i, carry):
            d = count // 2 + lax.div(i + 1, 2) * (2 * lax.rem(i, 2) - 1)
            other, device = peer(d)
            remote(send.at[other], recv.at[mine], device, sem).start()
            return carry

        lax.fori_loop(0, count - 1, step, 0)

    def keep(send, recv, mine):
        recv[mine] = send[mine]

    def spread(send, recv, mine, peer, count, sem):
        def step(i, carry):
            d = count // 2 + lax.div(i + 1, 2) * (2 * lax.rem(i, 2) - 1)
            remote(send, recv.at[mine], peer(d)[1], sem).start()
            return carry

        lax.fori_loop(0, count - 1, step, 0)
        recv[mine] = send[...]

    def arrive(recv, count, sem):
        part = recv.at[pl.ds(0, count - 1)]
        pltpu.make_async_copy(part, part, rsem.at[sem]).wait()

    def sent(send, count, sem):
        part = send.at[pl.ds(0, count - 1)]
        pltpu.make_async_copy(part, part, ssem.at[sem]).wait()

    def flat(ref, b):
        return ref[b].reshape(256, ROWS)

    def over_x(value, send, recv, b, sem):
        send[b] = value.astype(BF).reshape(NX, 32, ROWS)
        scatter(send.at[b], recv.at[b], mx, x_peer, NX, sem + b)
        keep(send.at[b], recv.at[b], mx)

    def over_l(value, send, recv, b, sem):
        send[b] = value.astype(BF).reshape(NL, 16, ROWS)
        scatter(send.at[b], recv.at[b], ml, l_peer, NL, sem + b)
        keep(send.at[b], recv.at[b], ml)

    zero_rows = jnp.zeros((BATCH, ROWS - CH, EXT), BF)
    xs[:, CH:ROWS, :] = zero_rows
    cs[:, CH:ROWS, :] = zero_rows
    kpad[...] = jnp.zeros_like(kpad)
    tables[0] = hot((256, 256), place0)
    tables[1] = hot((256, 256), place1)
    shift1 = hot((EXT, EXT), lambda r, c: r == c + 1)
    shift2 = hot((EXT, EXT), lambda r, c: r == c + 2)

    loads[0].wait()
    loads[1].wait()
    p0 = tables[0]
    for b in range(BATCH):
        m0 = nn(xs[b, :, 0:BLK], fs[0]).astype(BF)
        m1 = nn(xs[b, :, BLK:EXT], fs[1]).astype(BF)
        a0s[b] = (nt(p0[:, 0:BLK], m0) + nt(p0[:, BLK:EXT], m1)).astype(BF).reshape(NX, 32, ROWS)
    loads[2].wait()
    head = hot((16, EXT), lambda r, c: (r == c) & (r < 2))
    for b in range(BATCH):
        h0s[b] = nt(head, cs[b]).astype(BF)

    pl.semaphore_wait(barrier, NX - 1 + NL - 1 + CHAN - 1 + 2)

    halo0 = remote(h0s, h0r, (behind, chan), H0)
    halo0.start()
    for b in range(BATCH):
        scatter(a0s.at[b], a0r.at[b], mx, x_peer, NX, A0 + b)
        keep(a0s.at[b], a0r.at[b], mx)

    loads[3].wait()
    kpad[0:3, 0:CH] = kin[...]
    kcol[0:128, :] = kpad[:, 0:128].T
    kcol[128:256, :] = kpad[:, 128:256].T

    def gate_from(lanes, b, cot, near1, near2):
        near[0, b, :, lanes] = near1.astype(BF)
        near[1, b, :, lanes] = near2.astype(BF)
        value = kcol[:, 0:1] * cot.astype(F32) + kcol[:, 1:2] * near1 + kcol[:, 2:3] * near2
        gate[b, :, lanes] = value
        mgrad[b, :, lanes] = (value * xs[b, :, lanes].astype(F32)).astype(BF)

    last = NL - 1
    p1 = tables[1]
    for b in range(BATCH):
        gate_from(slice(0, EXT), b, cs[b], nn(cs[b], shift1), nn(cs[b], shift2))
        b1s[b] = nt(p1, mgrad[b]).astype(BF).reshape(NL, 16, ROWS)

        def step(i, carry):
            other, device = l_peer(NL // 2 + lax.div(i + 1, 2) * (2 * lax.rem(i, 2) - 1))

            @pl.when(other != last)
            def _():
                remote(b1s.at[b, other], b1r.at[b, ml], device, B1 + b).start()

            return carry

        lax.fori_loop(0, NL - 1, step, 0)

    tables[2] = hot((256, 256), turn0)
    arrive(a0r.at[0], NX, A0)
    over_l(nn(tables[2], flat(a0r, 0)), b0s, b0r, 0, B0)

    halo0.wait_recv()
    inside = (seq < SEQ - 1).astype(F32)
    high = slice(BLK, EXT)
    for b in range(BATCH):
        tail = (h0r[b].astype(F32) * inside).astype(BF)
        near1 = near[0, b, :, high].astype(F32)
        near2 = near[1, b, :, high].astype(F32)
        near1 = near1 + tn(tail, hot((16, BLK), lambda r, c: (r == 0) & (c == BLK - 1)))
        near2 = near2 + tn(tail, hot((16, BLK), lambda r, c: (r < 2) & (c == BLK - 2 + r)))
        gate_from(high, b, cs[b, :, high], near1, near2)
        b1s[b, last] = nt(tables[1, 16 * last : 16 * NL], mgrad[b]).astype(BF)

        @pl.when(ml != last)
        def _():
            remote(b1s.at[b, last], b1r.at[b, ml], (last * NX + mx, chan), B1 + b).start()

        keep(b1s.at[b], b1r.at[b], ml)

    arrive(a0r.at[1], NX, A0 + 1)
    over_l(nn(tables[2], flat(a0r, 1)), b0s, b0r, 1, B0)

    tables[3] = hot((256, 256), flip(turn0))
    tables[4] = hot((256, 256), turn1)
    tables[5] = hot((256, 256), flip(turn1))
    tables[6] = hot((256, 256), order1)
    loads[4].wait()
    eye = hot((256, 256), lambda r, c: r == c)
    second = sec[0]
    st[...] = nt(eye, second).astype(BF)
    back = hot((256, 256), flip(order1))
    s11[...] = nt(nn(back, second).astype(BF), back).astype(BF)

    for b in range(BATCH):
        xt[b] = nt(eye, xs[b]).astype(BF)
    for b in range(BATCH):
        arrive(b1r.at[b], NL, B1 + b)
        over_x(nn(tables[4], flat(b1r, b)), a1s, a1r, b, A1)
    for b in range(BATCH):
        arrive(b0r.at[b], NL, B0 + b)
        over_l(nn(st[...], flat(b0r, b)), b2s, b2r, b, B2)
    for b in range(BATCH):
        arrive(a1r.at[b], NX, A1 + b)
        over_x(nn(s11[...], flat(a1r, b)), a3s, a3r, b, A3)
    grad = jnp.zeros((256, 256), F32)
    for b in range(BATCH):
        nat = nn(tables[6], flat(a1r, b)).astype(BF)
        grad = grad + nt(flat(b0r, b), nat)
    fgo[...] = grad.reshape(CHAN, 64, 256)
    fgs[...] = grad.astype(BF).reshape(CHAN, 64, 256)
    for b in range(BATCH):
        arrive(b2r.at[b], NL, B2 + b)
        over_x(nn(tables[3], flat(b2r, b)), a2s, a2r, b, A2)
        arrive(a3r.at[b], NX, A3 + b)
        over_l(nn(tables[5], flat(a3r, b)), b3s, b3r, b, B3)
    scatter(fgs, fgr, chan, c_peer, CHAN, FG)

    edge = hot((16, EXT), lambda r, c: (r < 2) & (c == EXT - 2 + r))
    prods = [jnp.zeros((ROWS, BLK), F32)] * 3
    for b in range(BATCH):
        arrive(a2r.at[b], NX, A2 + b)
        monarch = tn(flat(a2r, b), tables[0])
        gated = (xs[b].astype(F32) * monarch).astype(BF)
        gat[b] = gated
        h1s[b] = nt(edge, gated).astype(BF)
        gate[b] = gate[b] * monarch
        gated32 = gated.astype(F32)
        for j in range(3):
            window = cs[b] if j == 0 else near[j - 1, b]
            prod = gated32 * window.astype(F32)
            prods[j] = prods[j] + (prod[:, 0:BLK] + prod[:, BLK:EXT])
    halo1 = remote(h1s, h1r, (ahead, chan), H1)
    halo1.start()
    sums = [jnp.sum(prod, axis=1, keepdims=True) for prod in prods]
    lane = lax.broadcasted_iota(jnp.int32, (ROWS, 128), 1)
    wide = jnp.where(lane == 0, sums[0], jnp.where(lane == 1, sums[1], sums[2]))
    kxs[:, 0:128] = wide[0:128].T[0:8]
    kxs[:, 128:256] = wide[128:256].T[0:8]
    spread(kxs, kxr, mx, x_peer, NX, KX)

    far1 = hot((EXT, EXT), lambda r, c: r + 1 == c)
    far2 = hot((EXT, EXT), lambda r, c: r + 2 == c)
    for b in range(BATCH):
        total[b] = (
            kcol[:, 0:1] * gat[b].astype(F32)
            + kcol[:, 1:2] * nn(gat[b], far1)
            + kcol[:, 2:3] * nn(gat[b], far2)
        )

    arrive(kxr, NX, KX)
    kls[...] = sum((kxr[i] for i in range(1, NX)), kxr[0])
    spread(kls, klr, ml, l_peer, NL, KL)

    for b in range(BATCH):
        arrive(b3r.at[b], NL, B3 + b)
        mgr[b] = tn(flat(b3r, b), tables[1]).astype(BF)
    for q in range(2):
        lanes = slice(q * BLK, (q + 1) * BLK)
        part = nn(xt[0, lanes, :], mgr[0, :, lanes]) + nn(xt[1, lanes, :], mgr[1, :, lanes])
        part = part.reshape(CHAN, 32, BLK)
        for o in range(CHAN):
            bgo[o, q] = part[o]
            bgs[o, q] = part[o].astype(BF)
    scatter(bgs, bgr, chan, c_peer, CHAN, BG)

    for q in range(2):
        lanes = slice(q * BLK, (q + 1) * BLK)
        for b in range(BATCH):
            through = nt(mgr[b, :, lanes], fs[q])
            igrad_ref[b, :, lanes] = (gate[b, :, lanes] + through)[0:CH].astype(BF)

    halo1.wait_recv()
    inside = (seq > 0).astype(F32)
    mixed_ref[:, :, high] = total[:, 0:CH, high].astype(BF)
    for b in range(BATCH):
        prior = (h1r[b].astype(F32) * inside).astype(BF)
        edge1 = tn(prior, hot((16, BLK), lambda r, c: (r == 1) & (c == 0)))
        edge2 = tn(prior, hot((16, BLK), lambda r, c: (r < 2) & (r == c)))
        value = total[b, :, 0:BLK] + (kcol[:, 1:2] * edge1 + kcol[:, 2:3] * edge2)
        mixed_ref[b, :, 0:BLK] = value[0:CH].astype(BF)

    arrive(fgr, CHAN, FG)
    fgr[chan] = jnp.zeros((64, 256), BF)
    got = [fgr[i].astype(F32) for i in range(CHAN)]
    fgrad_ref[0] = fgo[chan] + ((got[0] + got[1]) + (got[2] + got[3]))
    arrive(bgr, CHAN, BG)
    bgr[chan] = jnp.zeros((2, 32, BLK), BF)
    got = [bgr[i].astype(F32) for i in range(CHAN)]
    bgrad_ref[...] = bgo[chan] + ((got[0] + got[1]) + (got[2] + got[3]))
    arrive(klr, NL, KL)
    whole = sum((klr[i] for i in range(1, NL)), klr[0])
    kgrad_ref[...] = whole[0:3, 0:CH]

    halo0.wait_send()
    halo1.wait_send()
    for b in range(BATCH):
        for send, sem in ((a0s, A0), (a1s, A1), (a2s, A2), (a3s, A3)):
            sent(send.at[b], NX, sem + b)
        for send, sem in ((b0s, B0), (b1s, B1), (b2s, B2), (b3s, B3)):
            sent(send.at[b], NL, sem + b)
    sent(fgs, CHAN, FG)
    sent(bgs, CHAN, BG)
    sent(kxr, NX, KX)
    sent(klr, NL, KL)


def emit(*refs):
    ins, outs, held, sem = refs[0:5], refs[5:10], refs[10:15], refs[15]
    loads = [pltpu.make_async_copy(ins[i], held[i], sem.at[0, i]) for i in range(5)]
    stores = [pltpu.make_async_copy(held[i], outs[i], sem.at[1, i]) for i in range(5)]
    for load in loads:
        load.start()
    for load, store in zip(loads, stores):
        load.wait()
        store.start()
    for store in stores:
        store.wait()


def shards(inputs, first_blocks, second_blocks, kernel, cotangent):
    vmem = pl.BlockSpec(memory_space=pltpu.VMEM)
    free = pl.BlockSpec(memory_space=pl.ANY)
    xbuf = pltpu.VMEM((BATCH, NX, 32, ROWS), BF)
    lbuf = pltpu.VMEM((BATCH, NL, 16, ROWS), BF)
    halo = pltpu.VMEM((BATCH, 16, ROWS), BF)
    plane = pltpu.VMEM((BATCH, ROWS, EXT), BF)
    square = pltpu.VMEM((256, 256), BF)
    shapes = (
        jax.ShapeDtypeStruct((BATCH, CH, EXT), BF),
        jax.ShapeDtypeStruct((BATCH, CH, EXT), BF),
        jax.ShapeDtypeStruct((3, CH), F32),
        jax.ShapeDtypeStruct((2, BLK // CHAN, BLK), F32),
        jax.ShapeDtypeStruct((1, 256 // CHAN, 256), F32),
    )
    results = pl.pallas_call(
        body,
        out_shape=shapes,
        in_specs=[free] * 5,
        out_specs=(vmem,) * 5,
        scratch_shapes=[
            plane, plane,
            pltpu.VMEM((2, BLK, BLK), BF), pltpu.VMEM((1, 256, 256), BF),
            pltpu.VMEM((3, CH), F32), plane,
            pltpu.VMEM((BATCH, ROWS, EXT), F32), pltpu.VMEM((BATCH, ROWS, EXT), F32),
            plane, plane,
            pltpu.VMEM((2, BATCH, ROWS, EXT), BF),
            pltpu.VMEM((128, 256), F32), pltpu.VMEM((ROWS, 128), F32),
            square, square, plane,
            pltpu.VMEM((7, 256, 256), BF),
            xbuf, xbuf, lbuf, lbuf, lbuf, lbuf, xbuf, xbuf,
            lbuf, lbuf, xbuf, xbuf, xbuf, xbuf, lbuf, lbuf,
            halo, halo, halo, halo,
            pltpu.VMEM((8, 256), F32), pltpu.VMEM((NX, 8, 256), F32),
            pltpu.VMEM((8, 256), F32), pltpu.VMEM((NL, 8, 256), F32),
            pltpu.VMEM((CHAN, 64, 256), F32),
            pltpu.VMEM((CHAN, 64, 256), BF), pltpu.VMEM((CHAN, 64, 256), BF),
            pltpu.VMEM((CHAN, 2, 32, BLK), F32),
            pltpu.VMEM((CHAN, 2, 32, BLK), BF), pltpu.VMEM((CHAN, 2, 32, BLK), BF),
            pltpu.SemaphoreType.DMA((22,)),
            pltpu.SemaphoreType.DMA((22,)),
            pltpu.SemaphoreType.DMA((5,)),
        ],
        compiler_params=pltpu.CompilerParams(
            collective_id=0, has_side_effects=True, vmem_limit_bytes=60 * 1024 * 1024
        ),
    )(inputs, first_blocks, second_blocks, kernel, cotangent)
    return pl.pallas_call(
        emit,
        out_shape=shapes,
        in_specs=[free] * 5,
        out_specs=(free,) * 5,
        scratch_shapes=[pltpu.VMEM(one.shape, one.dtype) for one in shapes]
        + [pltpu.SemaphoreType.DMA((2, 5))],
        compiler_params=pltpu.CompilerParams(vmem_limit_bytes=60 * 1024 * 1024),
    )(*results)


def solution(mesh):
    placed = (
        P(None, "chan", "seq"),
        P("seq", None, None),
        P("seq", None, None),
        P(None, "chan"),
        P(None, "chan", "seq"),
    )
    return jax.shard_map(
        shards,
        mesh=mesh,
        in_specs=placed,
        out_specs=(
            P(None, "chan", "seq"),
            P(None, "chan", "seq"),
            P(None, "chan"),
            P("seq", "chan", None),
            P("seq", "chan", None),
        ),
        check_vma=False,
    )
```

```python
import jax
import jax.numpy as jnp
from jax import lax
from jax.experimental import pallas as pl
from jax.experimental.pallas import tpu as pltpu
from jax.sharding import PartitionSpec as P

NX, NL = 8, 16
SEQ, CHAN = NX * NL, 4
BATCH, CH, EXT, BLK = 2, 240, 256, 128
ROWS = 256
MESH = pl.DeviceIdType.MESH
BF, F32 = jnp.bfloat16, jnp.float32
A0, B0, B1, A1, B2, A2, A3, B3 = range(0, 16, 2)
FG, BG, KX, KL, H0, H1 = range(16, 22)


def dot(a, b, ca, cb):
    return lax.dot_general(a, b, (((ca,), (cb,)), ((), ())), preferred_element_type=F32)


def nn(a, b):
    return dot(a, b, 1, 0)


def nt(a, b):
    return dot(a, b, 1, 1)


def tn(a, b):
    return dot(a, b, 0, 0)


def hot(shape, where):
    row = lax.broadcasted_iota(jnp.int32, shape, 0)
    col = lax.broadcasted_iota(jnp.int32, shape, 1)
    return jnp.where(where(row, col), 1.0, 0.0).astype(BF)


def place0(r, c):
    return ((r >> 4) & 1) * 128 + (r & 15) * 8 + (r >> 5) == c


def turn0(r, c):
    return ((r >> 1) & 7) * 32 + (r & 1) * 16 + (r >> 4) == c


def place1(r, c):
    return ((r >> 3) & 1) * 128 + (r >> 4) * 8 + (r & 7) == c


def turn1(r, c):
    return ((r >> 1) & 15) * 16 + (r & 1) * 8 + (r >> 5) == c


def order1(r, c):
    return ((r >> 1) & 7) * 32 + (r >> 4) * 2 + (r & 1) == c


def flip(where):
    return lambda r, c: where(c, r)


def body(
    x_in, f_in, s_in, k_in, c_in,
    mixed_ref, igrad_ref, kgrad_ref, bgrad_ref, fgrad_ref,
    xs, cs, fs, sec, kin, xt, gate, total, gat, mon, mgrad, near, kpad, kcol, st, s11, mgr, tables,
    a0s, a0r, b0s, b0r, b1s, b1r, a1s, a1r,
    b2s, b2r, a2s, a2r, a3s, a3r, b3s, b3r,
    h0s, h0r, h1s, h1r,
    kxs, kxr, kls, klr, fgo, fgs, fgr, bgo, bgs, bgr,
    ssem, rsem, isem,
):
    seq = lax.axis_index("seq")
    chan = lax.axis_index("chan")
    mx = lax.rem(seq, NX)
    ml = lax.div(seq, NX)
    ahead = lax.rem(seq + 1, SEQ)
    behind = lax.rem(seq + SEQ - 1, SEQ)

    def x_peer(d):
        other = lax.rem(mx + d, NX)
        return other, (ml * NX + other, chan)

    def l_peer(d):
        other = lax.rem(ml + d, NL)
        return other, (other * NX + mx, chan)

    def c_peer(d):
        other = lax.rem(chan + d, CHAN)
        return other, (seq, other)

    barrier = pltpu.get_barrier_semaphore()

    def greet(peer, count):
        def step(d, carry):
            pl.semaphore_signal(barrier, inc=1, device_id=peer(d)[1], device_id_type=MESH)
            return carry

        lax.fori_loop(1, count, step, 0)

    loads = [
        pltpu.make_async_copy(c_in, cs.at[:, pl.ds(0, CH), :], isem.at[2]),
        pltpu.make_async_copy(x_in, xs.at[:, pl.ds(0, CH), :], isem.at[0]),
        pltpu.make_async_copy(f_in, fs, isem.at[1]),
        pltpu.make_async_copy(k_in, kin, isem.at[3]),
        pltpu.make_async_copy(s_in, sec, isem.at[4]),
    ]
    for load in loads:
        load.start()
    greet(x_peer, NX)
    greet(l_peer, NL)
    greet(c_peer, CHAN)
    pl.semaphore_signal(barrier, inc=1, device_id=(ahead, chan), device_id_type=MESH)
    pl.semaphore_signal(barrier, inc=1, device_id=(behind, chan), device_id_type=MESH)

    def remote(src, dst, device, sem):
        return pltpu.make_async_remote_copy(
            src_ref=src, dst_ref=dst, send_sem=ssem.at[sem], recv_sem=rsem.at[sem],
            device_id=device, device_id_type=MESH,
        )

    def scatter(send, recv, mine, peer, count, sem):
        def step(i, carry):
            d = count // 2 + lax.div(i + 1, 2) * (2 * lax.rem(i, 2) - 1)
            other, device = peer(d)
            remote(send.at[other], recv.at[mine], device, sem).start()
            return carry

        lax.fori_loop(0, count - 1, step, 0)

    def keep(send, recv, mine):
        recv[mine] = send[mine]

    def spread(send, recv, mine, peer, count, sem):
        def step(i, carry):
            d = count // 2 + lax.div(i + 1, 2) * (2 * lax.rem(i, 2) - 1)
            remote(send, recv.at[mine], peer(d)[1], sem).start()
            return carry

        lax.fori_loop(0, count - 1, step, 0)
        recv[mine] = send[...]

    def arrive(recv, count, sem):
        part = recv.at[pl.ds(0, count - 1)]
        pltpu.make_async_copy(part, part, rsem.at[sem]).wait()

    def sent(send, count, sem):
        part = send.at[pl.ds(0, count - 1)]
        pltpu.make_async_copy(part, part, ssem.at[sem]).wait()

    def flat(ref, b):
        return ref[b].reshape(256, ROWS)

    def over_x(value, send, recv, b, sem):
        send[b] = value.astype(BF).reshape(NX, 32, ROWS)
        scatter(send.at[b], recv.at[b], mx, x_peer, NX, sem + b)
        keep(send.at[b], recv.at[b], mx)

    def over_l(value, send, recv, b, sem):
        send[b] = value.astype(BF).reshape(NL, 16, ROWS)
        scatter(send.at[b], recv.at[b], ml, l_peer, NL, sem + b)
        keep(send.at[b], recv.at[b], ml)

    zero_rows = jnp.zeros((BATCH, ROWS - CH, EXT), BF)
    xs[:, CH:ROWS, :] = zero_rows
    cs[:, CH:ROWS, :] = zero_rows
    kpad[...] = jnp.zeros_like(kpad)
    tables[0] = hot((256, 256), place0)
    tables[1] = hot((256, 256), place1)
    shift1 = hot((EXT, EXT), lambda r, c: r == c + 1)
    shift2 = hot((EXT, EXT), lambda r, c: r == c + 2)

    loads[0].wait()
    head = hot((16, EXT), lambda r, c: (r == c) & (r < 2))
    for b in range(BATCH):
        h0s[b] = nt(head, cs[b]).astype(BF)

    pl.semaphore_wait(barrier, NX - 1 + NL - 1 + CHAN - 1 + 2)
    halo0 = remote(h0s, h0r, (behind, chan), H0)
    halo0.start()

    loads[1].wait()
    loads[2].wait()
    p0 = tables[0]
    for b in range(BATCH):
        m0 = nn(xs[b, :, 0:BLK], fs[0]).astype(BF)
        m1 = nn(xs[b, :, BLK:EXT], fs[1]).astype(BF)
        over_x(nt(p0[:, 0:BLK], m0) + nt(p0[:, BLK:EXT], m1), a0s, a0r, b, A0)

    loads[3].wait()
    kpad[0:3, 0:CH] = kin[...]
    kcol[0:128, :] = kpad[:, 0:128].T
    kcol[128:256, :] = kpad[:, 128:256].T

    def gate_from(lanes, b, cot, near1, near2):
        near[0, b, :, lanes] = near1.astype(BF)
        near[1, b, :, lanes] = near2.astype(BF)
        value = kcol[:, 0:1] * cot.astype(F32) + kcol[:, 1:2] * near1 + kcol[:, 2:3] * near2
        gate[b, :, lanes] = value
        mgrad[b, :, lanes] = (value * xs[b, :, lanes].astype(F32)).astype(BF)

    last = NL - 1
    p1 = tables[1]
    for b in range(BATCH):
        gate_from(slice(0, EXT), b, cs[b], nn(cs[b], shift1), nn(cs[b], shift2))
        b1s[b] = nt(p1, mgrad[b]).astype(BF).reshape(NL, 16, ROWS)

        def step(i, carry):
            other, device = l_peer(NL // 2 + lax.div(i + 1, 2) * (2 * lax.rem(i, 2) - 1))

            @pl.when(other != last)
            def _():
                remote(b1s.at[b, other], b1r.at[b, ml], device, B1 + b).start()

            return carry

        lax.fori_loop(0, NL - 1, step, 0)

    tables[2] = hot((256, 256), turn0)
    arrive(a0r.at[0], NX, A0)
    over_l(nn(tables[2], flat(a0r, 0)), b0s, b0r, 0, B0)

    halo0.wait_recv()
    inside = (seq < SEQ - 1).astype(F32)
    high = slice(BLK, EXT)
    for b in range(BATCH):
        tail = (h0r[b].astype(F32) * inside).astype(BF)
        near1 = near[0, b, :, high].astype(F32)
        near2 = near[1, b, :, high].astype(F32)
        near1 = near1 + tn(tail, hot((16, BLK), lambda r, c: (r == 0) & (c == BLK - 1)))
        near2 = near2 + tn(tail, hot((16, BLK), lambda r, c: (r < 2) & (c == BLK - 2 + r)))
        gate_from(high, b, cs[b, :, high], near1, near2)
        b1s[b, last] = nt(tables[1, 16 * last : 16 * NL], mgrad[b]).astype(BF)

        @pl.when(ml != last)
        def _():
            remote(b1s.at[b, last], b1r.at[b, ml], (last * NX + mx, chan), B1 + b).start()

        keep(b1s.at[b], b1r.at[b], ml)

    arrive(a0r.at[1], NX, A0 + 1)
    over_l(nn(tables[2], flat(a0r, 1)), b0s, b0r, 1, B0)

    tables[3] = hot((256, 256), flip(turn0))
    tables[4] = hot((256, 256), turn1)
    tables[5] = hot((256, 256), flip(turn1))
    tables[6] = hot((256, 256), order1)
    loads[4].wait()
    eye = hot((256, 256), lambda r, c: r == c)
    second = sec[0]
    st[...] = nt(eye, second).astype(BF)
    back = hot((256, 256), flip(order1))
    s11[...] = nt(nn(back, second).astype(BF), back).astype(BF)

    for b in range(BATCH):
        xt[b] = nt(eye, xs[b]).astype(BF)
    for b in range(BATCH):
        arrive(b1r.at[b], NL, B1 + b)
        over_x(nn(tables[4], flat(b1r, b)), a1s, a1r, b, A1)
    for b in range(BATCH):
        arrive(b0r.at[b], NL, B0 + b)
        over_l(nn(st[...], flat(b0r, b)), b2s, b2r, b, B2)
    for b in range(BATCH):
        arrive(a1r.at[b], NX, A1 + b)
        over_x(nn(s11[...], flat(a1r, b)), a3s, a3r, b, A3)
    grad = jnp.zeros((256, 256), F32)
    for b in range(BATCH):
        nat = nn(tables[6], flat(a1r, b)).astype(BF)
        grad = grad + nt(flat(b0r, b), nat)
    fgo[...] = grad.reshape(CHAN, 64, 256)
    fgs[...] = grad.astype(BF).reshape(CHAN, 64, 256)
    for b in range(BATCH):
        arrive(b2r.at[b], NL, B2 + b)
        over_x(nn(tables[3], flat(b2r, b)), a2s, a2r, b, A2)
        arrive(a3r.at[b], NX, A3 + b)
        over_l(nn(tables[5], flat(a3r, b)), b3s, b3r, b, B3)
    scatter(fgs, fgr, chan, c_peer, CHAN, FG)

    prods = [jnp.zeros((ROWS, BLK), F32)] * 3
    for b in range(BATCH):
        arrive(a2r.at[b], NX, A2 + b)
        monarch = tn(flat(a2r, b), tables[0])
        mon[b] = monarch.astype(BF)
        gated = (xs[b].astype(F32) * monarch).astype(BF)
        gat[b] = gated
        gated32 = gated.astype(F32)
        for j in range(3):
            window = cs[b] if j == 0 else near[j - 1, b]
            prod = gated32 * window.astype(F32)
            prods[j] = prods[j] + (prod[:, 0:BLK] + prod[:, BLK:EXT])
    sums = [jnp.sum(prod, axis=1, keepdims=True) for prod in prods]
    lane = lax.broadcasted_iota(jnp.int32, (ROWS, 128), 1)
    wide = jnp.where(lane == 0, sums[0], jnp.where(lane == 1, sums[1], sums[2]))
    kxs[:, 0:128] = wide[0:128].T[0:8]
    kxs[:, 128:256] = wide[128:256].T[0:8]
    spread(kxs, kxr, mx, x_peer, NX, KX)

    edge = hot((16, EXT), lambda r, c: (r < 2) & (c == EXT - 2 + r))
    for b in range(BATCH):
        h1s[b] = nt(edge, gat[b]).astype(BF)
    halo1 = remote(h1s, h1r, (ahead, chan), H1)
    halo1.start()

    for b in range(BATCH):
        arrive(b3r.at[b], NL, B3 + b)
        mgr[b] = tn(flat(b3r, b), tables[1]).astype(BF)
    for q in range(2):
        lanes = slice(q * BLK, (q + 1) * BLK)
        part = nn(xt[0, lanes, :], mgr[0, :, lanes]) + nn(xt[1, lanes, :], mgr[1, :, lanes])
        part = part.reshape(CHAN, 32, BLK)
        for o in range(CHAN):
            bgo[o, q] = part[o]
            bgs[o, q] = part[o].astype(BF)
    scatter(bgs, bgr, chan, c_peer, CHAN, BG)

    arrive(kxr, NX, KX)
    kls[...] = sum((kxr[i] for i in range(1, NX)), kxr[0])
    spread(kls, klr, ml, l_peer, NL, KL)

    far1 = hot((EXT, EXT), lambda r, c: r + 1 == c)
    far2 = hot((EXT, EXT), lambda r, c: r + 2 == c)
    for b in range(BATCH):
        total[b] = (
            kcol[:, 0:1] * gat[b].astype(F32)
            + kcol[:, 1:2] * nn(gat[b], far1)
            + kcol[:, 2:3] * nn(gat[b], far2)
        )
    for q in range(2):
        lanes = slice(q * BLK, (q + 1) * BLK)
        for b in range(BATCH):
            through = nt(mgr[b, :, lanes], fs[q])
            direct = gate[b, :, lanes] * mon[b, :, lanes].astype(F32)
            igrad_ref[b, :, lanes] = (direct + through)[0:CH].astype(BF)

    halo1.wait_recv()
    inside = (seq > 0).astype(F32)
    mixed_ref[:, :, high] = total[:, 0:CH, high].astype(BF)
    for b in range(BATCH):
        prior = (h1r[b].astype(F32) * inside).astype(BF)
        edge1 = tn(prior, hot((16, BLK), lambda r, c: (r == 1) & (c == 0)))
        edge2 = tn(prior, hot((16, BLK), lambda r, c: (r < 2) & (r == c)))
        value = total[b, :, 0:BLK] + (kcol[:, 1:2] * edge1 + kcol[:, 2:3] * edge2)
        mixed_ref[b, :, 0:BLK] = value[0:CH].astype(BF)

    arrive(fgr, CHAN, FG)
    fgr[chan] = jnp.zeros((64, 256), BF)
    got = [fgr[i].astype(F32) for i in range(CHAN)]
    fgrad_ref[0] = fgo[chan] + ((got[0] + got[1]) + (got[2] + got[3]))
    arrive(bgr, CHAN, BG)
    bgr[chan] = jnp.zeros((2, 32, BLK), BF)
    got = [bgr[i].astype(F32) for i in range(CHAN)]
    bgrad_ref[...] = bgo[chan] + ((got[0] + got[1]) + (got[2] + got[3]))
    arrive(klr, NL, KL)
    whole = sum((klr[i] for i in range(1, NL)), klr[0])
    kgrad_ref[...] = whole[0:3, 0:CH]

    halo0.wait_send()
    halo1.wait_send()
    for b in range(BATCH):
        for send, sem in ((a0s, A0), (a1s, A1), (a2s, A2), (a3s, A3)):
            sent(send.at[b], NX, sem + b)
        for send, sem in ((b0s, B0), (b1s, B1), (b2s, B2), (b3s, B3)):
            sent(send.at[b], NL, sem + b)
    sent(fgs, CHAN, FG)
    sent(bgs, CHAN, BG)
    sent(kxr, NX, KX)
    sent(klr, NL, KL)


def emit(*refs):
    ins, outs, held, sem = refs[0:5], refs[5:10], refs[10:15], refs[15]
    loads = [pltpu.make_async_copy(ins[i], held[i], sem.at[0, i]) for i in range(5)]
    stores = [pltpu.make_async_copy(held[i], outs[i], sem.at[1, i]) for i in range(5)]
    for load in loads:
        load.start()
    for load, store in zip(loads, stores):
        load.wait()
        store.start()
    for store in stores:
        store.wait()


def shards(inputs, first_blocks, second_blocks, kernel, cotangent):
    vmem = pl.BlockSpec(memory_space=pltpu.VMEM)
    free = pl.BlockSpec(memory_space=pl.ANY)
    xbuf = pltpu.VMEM((BATCH, NX, 32, ROWS), BF)
    lbuf = pltpu.VMEM((BATCH, NL, 16, ROWS), BF)
    halo = pltpu.VMEM((BATCH, 16, ROWS), BF)
    plane = pltpu.VMEM((BATCH, ROWS, EXT), BF)
    square = pltpu.VMEM((256, 256), BF)
    shapes = (
        jax.ShapeDtypeStruct((BATCH, CH, EXT), BF),
        jax.ShapeDtypeStruct((BATCH, CH, EXT), BF),
        jax.ShapeDtypeStruct((3, CH), F32),
        jax.ShapeDtypeStruct((2, BLK // CHAN, BLK), F32),
        jax.ShapeDtypeStruct((1, 256 // CHAN, 256), F32),
    )
    results = pl.pallas_call(
        body,
        out_shape=shapes,
        in_specs=[free] * 5,
        out_specs=(vmem,) * 5,
        scratch_shapes=[
            plane, plane,
            pltpu.VMEM((2, BLK, BLK), BF), pltpu.VMEM((1, 256, 256), BF),
            pltpu.VMEM((3, CH), F32), plane,
            pltpu.VMEM((BATCH, ROWS, EXT), F32), pltpu.VMEM((BATCH, ROWS, EXT), F32),
            plane, plane, plane,
            pltpu.VMEM((2, BATCH, ROWS, EXT), BF),
            pltpu.VMEM((128, 256), F32), pltpu.VMEM((ROWS, 128), F32),
            square, square, plane,
            pltpu.VMEM((7, 256, 256), BF),
            xbuf, xbuf, lbuf, lbuf, lbuf, lbuf, xbuf, xbuf,
            lbuf, lbuf, xbuf, xbuf, xbuf, xbuf, lbuf, lbuf,
            halo, halo, halo, halo,
            pltpu.VMEM((8, 256), F32), pltpu.VMEM((NX, 8, 256), F32),
            pltpu.VMEM((8, 256), F32), pltpu.VMEM((NL, 8, 256), F32),
            pltpu.VMEM((CHAN, 64, 256), F32),
            pltpu.VMEM((CHAN, 64, 256), BF), pltpu.VMEM((CHAN, 64, 256), BF),
            pltpu.VMEM((CHAN, 2, 32, BLK), F32),
            pltpu.VMEM((CHAN, 2, 32, BLK), BF), pltpu.VMEM((CHAN, 2, 32, BLK), BF),
            pltpu.SemaphoreType.DMA((22,)),
            pltpu.SemaphoreType.DMA((22,)),
            pltpu.SemaphoreType.DMA((5,)),
        ],
        compiler_params=pltpu.CompilerParams(
            collective_id=0, has_side_effects=True, vmem_limit_bytes=60 * 1024 * 1024
        ),
    )(inputs, first_blocks, second_blocks, kernel, cotangent)
    return pl.pallas_call(
        emit,
        out_shape=shapes,
        in_specs=[free] * 5,
        out_specs=(free,) * 5,
        scratch_shapes=[pltpu.VMEM(one.shape, one.dtype) for one in shapes]
        + [pltpu.SemaphoreType.DMA((2, 5))],
        compiler_params=pltpu.CompilerParams(vmem_limit_bytes=60 * 1024 * 1024),
    )(*results)


def solution(mesh):
    placed = (
        P(None, "chan", "seq"),
        P("seq", None, None),
        P("seq", None, None),
        P(None, "chan"),
        P(None, "chan", "seq"),
    )
    return jax.shard_map(
        shards,
        mesh=mesh,
        in_specs=placed,
        out_specs=(
            P(None, "chan", "seq"),
            P(None, "chan", "seq"),
            P(None, "chan"),
            P("seq", "chan", None),
            P("seq", "chan", None),
        ),
        check_vma=False,
    )
```

```python
import jax
import jax.numpy as jnp
from jax import lax
from jax.experimental import pallas as pl
from jax.experimental.pallas import tpu as pltpu
from jax.sharding import PartitionSpec as P

NX, NL = 8, 16
SEQ, CHAN = NX * NL, 4
BATCH, CH, EXT, BLK = 2, 240, 256, 128
ROWS = 256
MESH = pl.DeviceIdType.MESH
BF, F32 = jnp.bfloat16, jnp.float32
A0, B0, B1, A1, B2, A2, A3, B3 = range(0, 16, 2)
FG, BG, KX, KL, H0, H1 = range(16, 22)


def dot(a, b, ca, cb):
    return lax.dot_general(a, b, (((ca,), (cb,)), ((), ())), preferred_element_type=F32)


def nn(a, b):
    return dot(a, b, 1, 0)


def nt(a, b):
    return dot(a, b, 1, 1)


def tn(a, b):
    return dot(a, b, 0, 0)


def hot(shape, where):
    row = lax.broadcasted_iota(jnp.int32, shape, 0)
    col = lax.broadcasted_iota(jnp.int32, shape, 1)
    return jnp.where(where(row, col), 1.0, 0.0).astype(BF)


def place0(r, c):
    return ((r >> 4) & 1) * 128 + (r & 15) * 8 + (r >> 5) == c


def turn0(r, c):
    return ((r >> 1) & 7) * 32 + (r & 1) * 16 + (r >> 4) == c


def place1(r, c):
    return ((r >> 3) & 1) * 128 + (r >> 4) * 8 + (r & 7) == c


def turn1(r, c):
    return ((r >> 1) & 15) * 16 + (r & 1) * 8 + (r >> 5) == c


def order1(r, c):
    return ((r >> 1) & 7) * 32 + (r >> 4) * 2 + (r & 1) == c


def flip(where):
    return lambda r, c: where(c, r)


def body(
    x_in, f_in, s_in, k_in, c_in,
    mixed_out, igrad_out, kgrad_out, bgrad_out, fgrad_out,
    mixed_ref, igrad_ref, kgrad_ref, bgrad_ref, fgrad_ref,
    xs, cs, fs, sec, kin, xt, gate, total, gat, mon, mgrad, near, kpad, kcol, st, s11, mgr, tables,
    a0s, a0r, b0s, b0r, b1s, b1r, a1s, a1r,
    b2s, b2r, a2s, a2r, a3s, a3r, b3s, b3r,
    h0s, h0r, h1s, h1r,
    kxs, kxr, kls, klr, fgo, fgs, fgr, bgo, bgs, bgr,
    ssem, rsem, isem, osem,
):
    seq = lax.axis_index("seq")
    chan = lax.axis_index("chan")
    mx = lax.rem(seq, NX)
    ml = lax.div(seq, NX)
    ahead = lax.rem(seq + 1, SEQ)
    behind = lax.rem(seq + SEQ - 1, SEQ)

    def x_peer(d):
        other = lax.rem(mx + d, NX)
        return other, (ml * NX + other, chan)

    def l_peer(d):
        other = lax.rem(ml + d, NL)
        return other, (other * NX + mx, chan)

    def c_peer(d):
        other = lax.rem(chan + d, CHAN)
        return other, (seq, other)

    barrier = pltpu.get_barrier_semaphore()

    def greet(peer, count):
        def step(d, carry):
            pl.semaphore_signal(barrier, inc=1, device_id=peer(d)[1], device_id_type=MESH)
            return carry

        lax.fori_loop(1, count, step, 0)

    loads = [
        pltpu.make_async_copy(c_in, cs.at[:, pl.ds(0, CH), :], isem.at[2]),
        pltpu.make_async_copy(x_in, xs.at[:, pl.ds(0, CH), :], isem.at[0]),
        pltpu.make_async_copy(f_in, fs, isem.at[1]),
        pltpu.make_async_copy(k_in, kin, isem.at[3]),
        pltpu.make_async_copy(s_in, sec, isem.at[4]),
    ]
    for load in loads:
        load.start()
    greet(l_peer, NL)
    greet(x_peer, NX)
    greet(c_peer, CHAN)
    pl.semaphore_signal(barrier, inc=1, device_id=(ahead, chan), device_id_type=MESH)
    pl.semaphore_signal(barrier, inc=1, device_id=(behind, chan), device_id_type=MESH)

    def remote(src, dst, device, sem):
        return pltpu.make_async_remote_copy(
            src_ref=src, dst_ref=dst, send_sem=ssem.at[sem], recv_sem=rsem.at[sem],
            device_id=device, device_id_type=MESH,
        )

    def scatter(send, recv, mine, peer, count, sem):
        def step(i, carry):
            d = count // 2 + lax.div(i + 1, 2) * (2 * lax.rem(i, 2) - 1)
            other, device = peer(d)
            remote(send.at[other], recv.at[mine], device, sem).start()
            return carry

        lax.fori_loop(0, count - 1, step, 0)

    def keep(send, recv, mine):
        recv[mine] = send[mine]

    def spread(send, recv, mine, peer, count, sem):
        def step(i, carry):
            d = count // 2 + lax.div(i + 1, 2) * (2 * lax.rem(i, 2) - 1)
            remote(send, recv.at[mine], peer(d)[1], sem).start()
            return carry

        lax.fori_loop(0, count - 1, step, 0)
        recv[mine] = send[...]

    def arrive(recv, count, sem):
        part = recv.at[pl.ds(0, count - 1)]
        pltpu.make_async_copy(part, part, rsem.at[sem]).wait()

    def sent(send, count, sem):
        part = send.at[pl.ds(0, count - 1)]
        pltpu.make_async_copy(part, part, ssem.at[sem]).wait()

    def flat(ref, b):
        return ref[b].reshape(256, ROWS)

    def over_x(value, send, recv, b, sem):
        send[b] = value.astype(BF).reshape(NX, 32, ROWS)
        scatter(send.at[b], recv.at[b], mx, x_peer, NX, sem + b)
        keep(send.at[b], recv.at[b], mx)

    def over_l(value, send, recv, b, sem):
        send[b] = value.astype(BF).reshape(NL, 16, ROWS)
        scatter(send.at[b], recv.at[b], ml, l_peer, NL, sem + b)
        keep(send.at[b], recv.at[b], ml)

    zero_rows = jnp.zeros((BATCH, ROWS - CH, EXT), BF)
    xs[:, CH:ROWS, :] = zero_rows
    cs[:, CH:ROWS, :] = zero_rows
    kpad[...] = jnp.zeros_like(kpad)
    tables[0] = hot((256, 256), place0)
    tables[1] = hot((256, 256), place1)
    shift1 = hot((EXT, EXT), lambda r, c: r == c + 1)
    shift2 = hot((EXT, EXT), lambda r, c: r == c + 2)

    loads[0].wait()
    head = hot((16, EXT), lambda r, c: (r == c) & (r < 2))
    for b in range(BATCH):
        h0s[b] = nt(head, cs[b]).astype(BF)
    loads[1].wait()
    loads[2].wait()
    p0 = tables[0]
    for b in range(BATCH):
        m0 = nn(xs[b, :, 0:BLK], fs[0]).astype(BF)
        m1 = nn(xs[b, :, BLK:EXT], fs[1]).astype(BF)
        rows = nt(p0[:, 0:BLK], m0) + nt(p0[:, BLK:EXT], m1)
        a0s[b] = rows.astype(BF).reshape(NX, 32, ROWS)

    loads[3].wait()
    kpad[0:3, 0:CH] = kin[...]
    kcol[0:128, :] = kpad[:, 0:128].T
    kcol[128:256, :] = kpad[:, 128:256].T

    def gate_from(lanes, b, cot, near1, near2):
        near[0, b, :, lanes] = near1.astype(BF)
        near[1, b, :, lanes] = near2.astype(BF)
        value = kcol[:, 0:1] * cot.astype(F32) + kcol[:, 1:2] * near1 + kcol[:, 2:3] * near2
        gate[b, :, lanes] = value
        mgrad[b, :, lanes] = (value * xs[b, :, lanes].astype(F32)).astype(BF)

    last = NL - 1
    p1 = tables[1]
    for b in range(BATCH):
        gate_from(slice(0, EXT), b, cs[b], nn(cs[b], shift1), nn(cs[b], shift2))
        b1s[b] = nt(p1, mgrad[b]).astype(BF).reshape(NL, 16, ROWS)

    pl.semaphore_wait(barrier, NX - 1 + NL - 1 + CHAN - 1 + 2)

    halo0 = remote(h0s, h0r, (behind, chan), H0)
    halo0.start()
    for b in range(BATCH):
        scatter(a0s.at[b], a0r.at[b], mx, x_peer, NX, A0 + b)
    for b in range(BATCH):

        def step(i, carry):
            other, device = l_peer(NL // 2 + lax.div(i + 1, 2) * (2 * lax.rem(i, 2) - 1))

            @pl.when(other != last)
            def _():
                remote(b1s.at[b, other], b1r.at[b, ml], device, B1 + b).start()

            return carry

        lax.fori_loop(0, NL - 1, step, 0)
    for b in range(BATCH):
        keep(a0s.at[b], a0r.at[b], mx)

    tables[2] = hot((256, 256), turn0)
    tables[3] = hot((256, 256), flip(turn0))
    tables[4] = hot((256, 256), turn1)
    tables[5] = hot((256, 256), flip(turn1))
    tables[6] = hot((256, 256), order1)
    loads[4].wait()
    eye = hot((256, 256), lambda r, c: r == c)
    second = sec[0]
    st[...] = nt(eye, second).astype(BF)
    back = hot((256, 256), flip(order1))
    s11[...] = nt(nn(back, second).astype(BF), back).astype(BF)

    arrive(a0r.at[0], NX, A0)
    over_l(nn(tables[2], flat(a0r, 0)), b0s, b0r, 0, B0)

    halo0.wait_recv()
    inside = (seq < SEQ - 1).astype(F32)
    high = slice(BLK, EXT)
    for b in range(BATCH):
        tail = (h0r[b].astype(F32) * inside).astype(BF)
        near1 = near[0, b, :, high].astype(F32)
        near2 = near[1, b, :, high].astype(F32)
        near1 = near1 + tn(tail, hot((16, BLK), lambda r, c: (r == 0) & (c == BLK - 1)))
        near2 = near2 + tn(tail, hot((16, BLK), lambda r, c: (r < 2) & (c == BLK - 2 + r)))
        gate_from(high, b, cs[b, :, high], near1, near2)
        b1s[b, last] = nt(tables[1, 16 * last : 16 * NL], mgrad[b]).astype(BF)

        @pl.when(ml != last)
        def _():
            remote(b1s.at[b, last], b1r.at[b, ml], (last * NX + mx, chan), B1 + b).start()

        keep(b1s.at[b], b1r.at[b], ml)

    arrive(a0r.at[1], NX, A0 + 1)
    over_l(nn(tables[2], flat(a0r, 1)), b0s, b0r, 1, B0)

    for b in range(BATCH):
        xt[b] = nt(eye, xs[b]).astype(BF)
    for b in range(BATCH):
        arrive(b1r.at[b], NL, B1 + b)
        over_x(nn(tables[4], flat(b1r, b)), a1s, a1r, b, A1)
    for b in range(BATCH):
        arrive(b0r.at[b], NL, B0 + b)
        over_l(nn(st[...], flat(b0r, b)), b2s, b2r, b, B2)
    for b in range(BATCH):
        arrive(a1r.at[b], NX, A1 + b)
        over_x(nn(s11[...], flat(a1r, b)), a3s, a3r, b, A3)
    grad = jnp.zeros((256, 256), F32)
    for b in range(BATCH):
        nat = nn(tables[6], flat(a1r, b)).astype(BF)
        grad = grad + nt(flat(b0r, b), nat)
    fgo[...] = grad.reshape(CHAN, 64, 256)
    fgs[...] = grad.astype(BF).reshape(CHAN, 64, 256)
    for b in range(BATCH):
        arrive(b2r.at[b], NL, B2 + b)
        over_x(nn(tables[3], flat(b2r, b)), a2s, a2r, b, A2)
        arrive(a3r.at[b], NX, A3 + b)
        over_l(nn(tables[5], flat(a3r, b)), b3s, b3r, b, B3)
    scatter(fgs, fgr, chan, c_peer, CHAN, FG)

    prods = [jnp.zeros((ROWS, BLK), F32)] * 3
    for b in range(BATCH):
        arrive(a2r.at[b], NX, A2 + b)
        monarch = tn(flat(a2r, b), tables[0])
        mon[b] = monarch.astype(BF)
        gated = (xs[b].astype(F32) * monarch).astype(BF)
        gat[b] = gated
        gated32 = gated.astype(F32)
        for j in range(3):
            window = cs[b] if j == 0 else near[j - 1, b]
            prod = gated32 * window.astype(F32)
            prods[j] = prods[j] + (prod[:, 0:BLK] + prod[:, BLK:EXT])
    sums = [jnp.sum(prod, axis=1, keepdims=True) for prod in prods]
    lane = lax.broadcasted_iota(jnp.int32, (ROWS, 128), 1)
    wide = jnp.where(lane == 0, sums[0], jnp.where(lane == 1, sums[1], sums[2]))
    kxs[:, 0:128] = wide[0:128].T[0:8]
    kxs[:, 128:256] = wide[128:256].T[0:8]
    spread(kxs, kxr, mx, x_peer, NX, KX)

    edge = hot((16, EXT), lambda r, c: (r < 2) & (c == EXT - 2 + r))
    for b in range(BATCH):
        h1s[b] = nt(edge, gat[b]).astype(BF)
    halo1 = remote(h1s, h1r, (ahead, chan), H1)
    halo1.start()

    for b in range(BATCH):
        arrive(b3r.at[b], NL, B3 + b)
        mgr[b] = tn(flat(b3r, b), tables[1]).astype(BF)
    for q in range(2):
        lanes = slice(q * BLK, (q + 1) * BLK)
        part = nn(xt[0, lanes, :], mgr[0, :, lanes]) + nn(xt[1, lanes, :], mgr[1, :, lanes])
        part = part.reshape(CHAN, 32, BLK)
        for o in range(CHAN):
            bgo[o, q] = part[o]
            bgs[o, q] = part[o].astype(BF)
    scatter(bgs, bgr, chan, c_peer, CHAN, BG)

    arrive(kxr, NX, KX)
    kls[...] = sum((kxr[i] for i in range(1, NX)), kxr[0])
    spread(kls, klr, ml, l_peer, NL, KL)

    far1 = hot((EXT, EXT), lambda r, c: r + 1 == c)
    far2 = hot((EXT, EXT), lambda r, c: r + 2 == c)
    for b in range(BATCH):
        total[b] = (
            kcol[:, 0:1] * gat[b].astype(F32)
            + kcol[:, 1:2] * nn(gat[b], far1)
            + kcol[:, 2:3] * nn(gat[b], far2)
        )
    for q in range(2):
        lanes = slice(q * BLK, (q + 1) * BLK)
        for b in range(BATCH):
            through = nt(mgr[b, :, lanes], fs[q])
            direct = gate[b, :, lanes] * mon[b, :, lanes].astype(F32)
            igrad_ref[b, :, lanes] = (direct + through)[0:CH].astype(BF)

    stores = [
        pltpu.make_async_copy(igrad_ref, igrad_out, osem.at[0]),
        pltpu.make_async_copy(mixed_ref, mixed_out, osem.at[1]),
        pltpu.make_async_copy(fgrad_ref, fgrad_out, osem.at[2]),
        pltpu.make_async_copy(bgrad_ref, bgrad_out, osem.at[3]),
        pltpu.make_async_copy(kgrad_ref, kgrad_out, osem.at[4]),
    ]
    stores[0].start()

    halo1.wait_recv()
    inside = (seq > 0).astype(F32)
    mixed_ref[:, :, high] = total[:, 0:CH, high].astype(BF)
    for b in range(BATCH):
        prior = (h1r[b].astype(F32) * inside).astype(BF)
        edge1 = tn(prior, hot((16, BLK), lambda r, c: (r == 1) & (c == 0)))
        edge2 = tn(prior, hot((16, BLK), lambda r, c: (r < 2) & (r == c)))
        value = total[b, :, 0:BLK] + (kcol[:, 1:2] * edge1 + kcol[:, 2:3] * edge2)
        mixed_ref[b, :, 0:BLK] = value[0:CH].astype(BF)
    stores[1].start()

    arrive(fgr, CHAN, FG)
    fgr[chan] = jnp.zeros((64, 256), BF)
    got = [fgr[i].astype(F32) for i in range(CHAN)]
    fgrad_ref[0] = fgo[chan] + ((got[0] + got[1]) + (got[2] + got[3]))
    stores[2].start()
    arrive(bgr, CHAN, BG)
    bgr[chan] = jnp.zeros((2, 32, BLK), BF)
    got = [bgr[i].astype(F32) for i in range(CHAN)]
    bgrad_ref[...] = bgo[chan] + ((got[0] + got[1]) + (got[2] + got[3]))
    stores[3].start()
    arrive(klr, NL, KL)
    whole = sum((klr[i] for i in range(1, NL)), klr[0])
    kgrad_ref[...] = whole[0:3, 0:CH]
    stores[4].start()

    halo0.wait_send()
    halo1.wait_send()
    for b in range(BATCH):
        for send, sem in ((a0s, A0), (a1s, A1), (a2s, A2), (a3s, A3)):
            sent(send.at[b], NX, sem + b)
        for send, sem in ((b0s, B0), (b1s, B1), (b2s, B2), (b3s, B3)):
            sent(send.at[b], NL, sem + b)
    sent(fgs, CHAN, FG)
    sent(bgs, CHAN, BG)
    sent(kxr, NX, KX)
    sent(klr, NL, KL)
    for store in stores:
        store.wait()


def emit(*refs):
    ins, outs, held, sem = refs[0:5], refs[5:10], refs[10:15], refs[15]
    loads = [pltpu.make_async_copy(ins[i], held[i], sem.at[0, i]) for i in range(5)]
    stores = [pltpu.make_async_copy(held[i], outs[i], sem.at[1, i]) for i in range(5)]
    for load in loads:
        load.start()
    for load, store in zip(loads, stores):
        load.wait()
        store.start()
    for store in stores:
        store.wait()


def shards(inputs, first_blocks, second_blocks, kernel, cotangent):
    free = pl.BlockSpec(memory_space=pl.ANY)
    xbuf = pltpu.VMEM((BATCH, NX, 32, ROWS), BF)
    lbuf = pltpu.VMEM((BATCH, NL, 16, ROWS), BF)
    halo = pltpu.VMEM((BATCH, 16, ROWS), BF)
    plane = pltpu.VMEM((BATCH, ROWS, EXT), BF)
    square = pltpu.VMEM((256, 256), BF)
    shapes = (
        jax.ShapeDtypeStruct((BATCH, CH, EXT), BF),
        jax.ShapeDtypeStruct((BATCH, CH, EXT), BF),
        jax.ShapeDtypeStruct((3, CH), F32),
        jax.ShapeDtypeStruct((2, BLK // CHAN, BLK), F32),
        jax.ShapeDtypeStruct((1, 256 // CHAN, 256), F32),
    )
    results = pl.pallas_call(
        body,
        out_shape=shapes,
        in_specs=[free] * 5,
        out_specs=(free,) * 5,
        scratch_shapes=[pltpu.VMEM(one.shape, one.dtype) for one in shapes]
        + [
            plane, plane,
            pltpu.VMEM((2, BLK, BLK), BF), pltpu.VMEM((1, 256, 256), BF),
            pltpu.VMEM((3, CH), F32), plane,
            pltpu.VMEM((BATCH, ROWS, EXT), F32), pltpu.VMEM((BATCH, ROWS, EXT), F32),
            plane, plane, plane,
            pltpu.VMEM((2, BATCH, ROWS, EXT), BF),
            pltpu.VMEM((128, 256), F32), pltpu.VMEM((ROWS, 128), F32),
            square, square, plane,
            pltpu.VMEM((7, 256, 256), BF),
            xbuf, xbuf, lbuf, lbuf, lbuf, lbuf, xbuf, xbuf,
            lbuf, lbuf, xbuf, xbuf, xbuf, xbuf, lbuf, lbuf,
            halo, halo, halo, halo,
            pltpu.VMEM((8, 256), F32), pltpu.VMEM((NX, 8, 256), F32),
            pltpu.VMEM((8, 256), F32), pltpu.VMEM((NL, 8, 256), F32),
            pltpu.VMEM((CHAN, 64, 256), F32),
            pltpu.VMEM((CHAN, 64, 256), BF), pltpu.VMEM((CHAN, 64, 256), BF),
            pltpu.VMEM((CHAN, 2, 32, BLK), F32),
            pltpu.VMEM((CHAN, 2, 32, BLK), BF), pltpu.VMEM((CHAN, 2, 32, BLK), BF),
            pltpu.SemaphoreType.DMA((22,)),
            pltpu.SemaphoreType.DMA((22,)),
            pltpu.SemaphoreType.DMA((5,)),
            pltpu.SemaphoreType.DMA((5,)),
        ],
        compiler_params=pltpu.CompilerParams(
            collective_id=0, has_side_effects=True, vmem_limit_bytes=60 * 1024 * 1024
        ),
    )(inputs, first_blocks, second_blocks, kernel, cotangent)
    return pl.pallas_call(
        emit,
        out_shape=shapes,
        in_specs=[free] * 5,
        out_specs=(free,) * 5,
        scratch_shapes=[pltpu.VMEM(one.shape, one.dtype) for one in shapes]
        + [pltpu.SemaphoreType.DMA((2, 5))],
        compiler_params=pltpu.CompilerParams(vmem_limit_bytes=60 * 1024 * 1024),
    )(*results)


def solution(mesh):
    placed = (
        P(None, "chan", "seq"),
        P("seq", None, None),
        P("seq", None, None),
        P(None, "chan"),
        P(None, "chan", "seq"),
    )
    return jax.shard_map(
        shards,
        mesh=mesh,
        in_specs=placed,
        out_specs=(
            P(None, "chan", "seq"),
            P(None, "chan", "seq"),
            P(None, "chan"),
            P("seq", "chan", None),
            P("seq", "chan", None),
        ),
        check_vma=False,
    )
```

```python
import jax
import jax.numpy as jnp
from jax import lax
from jax.experimental import pallas as pl
from jax.experimental.pallas import tpu as pltpu
from jax.sharding import PartitionSpec as P

NX, NL = 8, 16
SEQ, CHAN = NX * NL, 4
BATCH, CH, EXT, BLK = 2, 240, 256, 128
ROWS = 256
MESH = pl.DeviceIdType.MESH
BF, F32 = jnp.bfloat16, jnp.float32
A0, B0, B1, A1, B2, A2, A3, B3 = range(0, 16, 2)
FG, FH, BG, KX, KL, H0, H1 = range(16, 23)


def dot(a, b, ca, cb):
    return lax.dot_general(a, b, (((ca,), (cb,)), ((), ())), preferred_element_type=F32)


def nn(a, b):
    return dot(a, b, 1, 0)


def nt(a, b):
    return dot(a, b, 1, 1)


def tn(a, b):
    return dot(a, b, 0, 0)


def hot(shape, where):
    row = lax.broadcasted_iota(jnp.int32, shape, 0)
    col = lax.broadcasted_iota(jnp.int32, shape, 1)
    return jnp.where(where(row, col), 1.0, 0.0).astype(BF)


def place0(r, c):
    return ((r >> 4) & 1) * 128 + (r & 15) * 8 + (r >> 5) == c


def turn0(r, c):
    return ((r >> 1) & 7) * 32 + (r & 1) * 16 + (r >> 4) == c


def place1(r, c):
    return ((r >> 3) & 1) * 128 + (r >> 4) * 8 + (r & 7) == c


def turn1(r, c):
    return ((r >> 1) & 15) * 16 + (r & 1) * 8 + (r >> 5) == c


def order1(r, c):
    return ((r >> 1) & 7) * 32 + (r >> 4) * 2 + (r & 1) == c


def flip(where):
    return lambda r, c: where(c, r)


def body(
    x_in, f_in, s_in, k_in, c_in,
    mixed_out, igrad_out, kgrad_out, bgrad_out, fgrad_out,
    mixed_ref, igrad_ref, kgrad_ref, bgrad_ref, fgrad_ref,
    xs, cs, fs, sec, kin, xt, gate, total, gat, mon, mgrad, near, kpad, kcol, st, s11, mgr, tables,
    a0s, a0r, b0s, b0r, b1s, b1r, a1s, a1r,
    b2s, b2r, a2s, a2r, a3s, a3r, b3s, b3r,
    h0s, h0r, h1s, h1r,
    kxs, kxr, kls, klr, fgo, fgp, fgs, fgr, bgo, bgs, bgr,
    ssem, rsem, isem, osem,
):
    seq = lax.axis_index("seq")
    chan = lax.axis_index("chan")
    mx = lax.rem(seq, NX)
    ml = lax.div(seq, NX)
    ahead = lax.rem(seq + 1, SEQ)
    behind = lax.rem(seq + SEQ - 1, SEQ)

    def x_peer(d):
        other = lax.rem(mx + d, NX)
        return other, (ml * NX + other, chan)

    def l_peer(d):
        other = lax.rem(ml + d, NL)
        return other, (other * NX + mx, chan)

    def c_peer(d):
        other = lax.rem(chan + d, CHAN)
        return other, (seq, other)

    barrier = pltpu.get_barrier_semaphore()

    def greet(peer, count):
        def step(d, carry):
            pl.semaphore_signal(barrier, inc=1, device_id=peer(d)[1], device_id_type=MESH)
            return carry

        lax.fori_loop(1, count, step, 0)

    loads = [
        pltpu.make_async_copy(c_in, cs.at[:, pl.ds(0, CH), :], isem.at[2]),
        pltpu.make_async_copy(x_in, xs.at[:, pl.ds(0, CH), :], isem.at[0]),
        pltpu.make_async_copy(f_in, fs, isem.at[1]),
        pltpu.make_async_copy(k_in, kin, isem.at[3]),
        pltpu.make_async_copy(s_in, sec, isem.at[4]),
    ]
    for load in loads:
        load.start()
    greet(l_peer, NL)
    greet(x_peer, NX)
    greet(c_peer, CHAN)
    pl.semaphore_signal(barrier, inc=1, device_id=(ahead, chan), device_id_type=MESH)
    pl.semaphore_signal(barrier, inc=1, device_id=(behind, chan), device_id_type=MESH)

    def remote(src, dst, device, sem):
        return pltpu.make_async_remote_copy(
            src_ref=src, dst_ref=dst, send_sem=ssem.at[sem], recv_sem=rsem.at[sem],
            device_id=device, device_id_type=MESH,
        )

    def scatter(send, recv, mine, peer, count, sem):
        def step(i, carry):
            d = count // 2 + lax.div(i + 1, 2) * (2 * lax.rem(i, 2) - 1)
            other, device = peer(d)
            remote(send.at[other], recv.at[mine], device, sem).start()
            return carry

        lax.fori_loop(0, count - 1, step, 0)

    def keep(send, recv, mine):
        recv[mine] = send[mine]

    def spread(send, recv, mine, peer, count, sem):
        def step(i, carry):
            d = count // 2 + lax.div(i + 1, 2) * (2 * lax.rem(i, 2) - 1)
            remote(send, recv.at[mine], peer(d)[1], sem).start()
            return carry

        lax.fori_loop(0, count - 1, step, 0)
        recv[mine] = send[...]

    def arrive(recv, count, sem):
        part = recv.at[pl.ds(0, count - 1)]
        pltpu.make_async_copy(part, part, rsem.at[sem]).wait()

    def sent(send, count, sem):
        part = send.at[pl.ds(0, count - 1)]
        pltpu.make_async_copy(part, part, ssem.at[sem]).wait()

    def flat(ref, b):
        return ref[b].reshape(256, ROWS)

    def over_x(value, send, recv, b, sem):
        send[b] = value.astype(BF).reshape(NX, 32, ROWS)
        scatter(send.at[b], recv.at[b], mx, x_peer, NX, sem + b)
        keep(send.at[b], recv.at[b], mx)

    def over_l(value, send, recv, b, sem):
        send[b] = value.astype(BF).reshape(NL, 16, ROWS)
        scatter(send.at[b], recv.at[b], ml, l_peer, NL, sem + b)
        keep(send.at[b], recv.at[b], ml)

    zero_rows = jnp.zeros((BATCH, ROWS - CH, EXT), BF)
    xs[:, CH:ROWS, :] = zero_rows
    cs[:, CH:ROWS, :] = zero_rows
    kpad[...] = jnp.zeros_like(kpad)
    tables[0] = hot((256, 256), place0)
    tables[1] = hot((256, 256), place1)
    shift1 = hot((EXT, EXT), lambda r, c: r == c + 1)
    shift2 = hot((EXT, EXT), lambda r, c: r == c + 2)

    loads[0].wait()
    head = hot((16, EXT), lambda r, c: (r == c) & (r < 2))
    for b in range(BATCH):
        h0s[b] = nt(head, cs[b]).astype(BF)
    loads[1].wait()
    loads[2].wait()
    p0 = tables[0]
    for b in range(BATCH):
        m0 = nn(xs[b, :, 0:BLK], fs[0]).astype(BF)
        m1 = nn(xs[b, :, BLK:EXT], fs[1]).astype(BF)
        rows = nt(p0[:, 0:BLK], m0) + nt(p0[:, BLK:EXT], m1)
        a0s[b] = rows.astype(BF).reshape(NX, 32, ROWS)

    loads[3].wait()
    kpad[0:3, 0:CH] = kin[...]
    kcol[0:128, :] = kpad[:, 0:128].T
    kcol[128:256, :] = kpad[:, 128:256].T

    def gate_from(lanes, b, cot, near1, near2):
        near[0, b, :, lanes] = near1.astype(BF)
        near[1, b, :, lanes] = near2.astype(BF)
        value = kcol[:, 0:1] * cot.astype(F32) + kcol[:, 1:2] * near1 + kcol[:, 2:3] * near2
        gate[b, :, lanes] = value
        mgrad[b, :, lanes] = (value * xs[b, :, lanes].astype(F32)).astype(BF)

    last = NL - 1
    p1 = tables[1]
    for b in range(BATCH):
        gate_from(slice(0, EXT), b, cs[b], nn(cs[b], shift1), nn(cs[b], shift2))
        b1s[b] = nt(p1, mgrad[b]).astype(BF).reshape(NL, 16, ROWS)

    pl.semaphore_wait(barrier, NX - 1 + NL - 1 + CHAN - 1 + 2)

    halo0 = remote(h0s, h0r, (behind, chan), H0)
    halo0.start()
    for b in range(BATCH):
        scatter(a0s.at[b], a0r.at[b], mx, x_peer, NX, A0 + b)
    for b in range(BATCH):

        def step(i, carry):
            other, device = l_peer(NL // 2 + lax.div(i + 1, 2) * (2 * lax.rem(i, 2) - 1))

            @pl.when(other != last)
            def _():
                remote(b1s.at[b, other], b1r.at[b, ml], device, B1 + b).start()

            return carry

        lax.fori_loop(0, NL - 1, step, 0)
    for b in range(BATCH):
        keep(a0s.at[b], a0r.at[b], mx)

    tables[2] = hot((256, 256), turn0)
    tables[3] = hot((256, 256), flip(turn0))
    tables[4] = hot((256, 256), turn1)
    tables[5] = hot((256, 256), flip(turn1))
    tables[6] = hot((256, 256), order1)
    loads[4].wait()
    eye = hot((256, 256), lambda r, c: r == c)
    second = sec[0]
    st[...] = nt(eye, second).astype(BF)
    back = hot((256, 256), flip(order1))
    s11[...] = nt(nn(back, second).astype(BF), back).astype(BF)

    arrive(a0r.at[0], NX, A0)
    over_l(nn(tables[2], flat(a0r, 0)), b0s, b0r, 0, B0)

    halo0.wait_recv()
    inside = (seq < SEQ - 1).astype(F32)
    high = slice(BLK, EXT)
    for b in range(BATCH):
        tail = (h0r[b].astype(F32) * inside).astype(BF)
        near1 = near[0, b, :, high].astype(F32)
        near2 = near[1, b, :, high].astype(F32)
        near1 = near1 + tn(tail, hot((16, BLK), lambda r, c: (r == 0) & (c == BLK - 1)))
        near2 = near2 + tn(tail, hot((16, BLK), lambda r, c: (r < 2) & (c == BLK - 2 + r)))
        gate_from(high, b, cs[b, :, high], near1, near2)
        b1s[b, last] = nt(tables[1, 16 * last : 16 * NL], mgrad[b]).astype(BF)

        @pl.when(ml != last)
        def _():
            remote(b1s.at[b, last], b1r.at[b, ml], (last * NX + mx, chan), B1 + b).start()

        keep(b1s.at[b], b1r.at[b], ml)

    arrive(a0r.at[1], NX, A0 + 1)
    over_l(nn(tables[2], flat(a0r, 1)), b0s, b0r, 1, B0)

    for b in range(BATCH):
        xt[b] = nt(eye, xs[b]).astype(BF)
    for b in range(BATCH):
        arrive(b1r.at[b], NL, B1 + b)
        over_x(nn(tables[4], flat(b1r, b)), a1s, a1r, b, A1)
    for b in range(BATCH):
        arrive(b0r.at[b], NL, B0 + b)
        over_l(nn(st[...], flat(b0r, b)), b2s, b2r, b, B2)
    for b in range(BATCH):
        arrive(a1r.at[b], NX, A1 + b)
        over_x(nn(s11[...], flat(a1r, b)), a3s, a3r, b, A3)
    grad = jnp.zeros((256, 256), F32)
    for b in range(BATCH):
        nat = nn(tables[6], flat(a1r, b)).astype(BF)
        grad = grad + nt(flat(b0r, b), nat)
    fgo[...] = grad.reshape(CHAN, 64, 256)
    core = lax.rem(chan, 2)
    half = lax.div(chan, 2)
    for h in range(2):
        remote(fgo.at[2 * h + 1 - core], fgp.at[h], (seq, 2 * half + 1 - core), FG).start()
    for b in range(BATCH):
        arrive(b2r.at[b], NL, B2 + b)
        over_x(nn(tables[3], flat(b2r, b)), a2s, a2r, b, A2)
        arrive(a3r.at[b], NX, A3 + b)
        over_l(nn(tables[5], flat(a3r, b)), b3s, b3r, b, B3)
    pltpu.make_async_copy(fgp, fgp, rsem.at[FG]).wait()
    fgs[...] = (fgo[2 * (1 - half) + core] + fgp[1 - half]).astype(BF)
    pair = remote(fgs, fgr, (seq, 2 * (1 - half) + core), FH)
    pair.start()

    prods = [jnp.zeros((ROWS, BLK), F32)] * 3
    for b in range(BATCH):
        arrive(a2r.at[b], NX, A2 + b)
        monarch = tn(flat(a2r, b), tables[0])
        mon[b] = monarch.astype(BF)
        gated = (xs[b].astype(F32) * monarch).astype(BF)
        gat[b] = gated
        gated32 = gated.astype(F32)
        for j in range(3):
            window = cs[b] if j == 0 else near[j - 1, b]
            prod = gated32 * window.astype(F32)
            prods[j] = prods[j] + (prod[:, 0:BLK] + prod[:, BLK:EXT])
    sums = [jnp.sum(prod, axis=1, keepdims=True) for prod in prods]
    lane = lax.broadcasted_iota(jnp.int32, (ROWS, 128), 1)
    wide = jnp.where(lane == 0, sums[0], jnp.where(lane == 1, sums[1], sums[2]))
    kxs[:, 0:128] = wide[0:128].T[0:8]
    kxs[:, 128:256] = wide[128:256].T[0:8]
    spread(kxs, kxr, mx, x_peer, NX, KX)

    edge = hot((16, EXT), lambda r, c: (r < 2) & (c == EXT - 2 + r))
    for b in range(BATCH):
        h1s[b] = nt(edge, gat[b]).astype(BF)
    halo1 = remote(h1s, h1r, (ahead, chan), H1)
    halo1.start()

    for b in range(BATCH):
        arrive(b3r.at[b], NL, B3 + b)
        mgr[b] = tn(flat(b3r, b), tables[1]).astype(BF)
    for q in range(2):
        lanes = slice(q * BLK, (q + 1) * BLK)
        part = nn(xt[0, lanes, :], mgr[0, :, lanes]) + nn(xt[1, lanes, :], mgr[1, :, lanes])
        part = part.reshape(CHAN, 32, BLK)
        for o in range(CHAN):
            bgo[o, q] = part[o]
            bgs[o, q] = part[o].astype(BF)
    scatter(bgs, bgr, chan, c_peer, CHAN, BG)

    arrive(kxr, NX, KX)
    kls[...] = sum((kxr[i] for i in range(1, NX)), kxr[0])
    spread(kls, klr, ml, l_peer, NL, KL)

    far1 = hot((EXT, EXT), lambda r, c: r + 1 == c)
    far2 = hot((EXT, EXT), lambda r, c: r + 2 == c)
    for b in range(BATCH):
        total[b] = (
            kcol[:, 0:1] * gat[b].astype(F32)
            + kcol[:, 1:2] * nn(gat[b], far1)
            + kcol[:, 2:3] * nn(gat[b], far2)
        )
    for q in range(2):
        lanes = slice(q * BLK, (q + 1) * BLK)
        for b in range(BATCH):
            through = nt(mgr[b, :, lanes], fs[q])
            direct = gate[b, :, lanes] * mon[b, :, lanes].astype(F32)
            igrad_ref[b, :, lanes] = (direct + through)[0:CH].astype(BF)

    stores = [
        pltpu.make_async_copy(igrad_ref, igrad_out, osem.at[0]),
        pltpu.make_async_copy(mixed_ref, mixed_out, osem.at[1]),
        pltpu.make_async_copy(fgrad_ref, fgrad_out, osem.at[2]),
        pltpu.make_async_copy(bgrad_ref, bgrad_out, osem.at[3]),
        pltpu.make_async_copy(kgrad_ref, kgrad_out, osem.at[4]),
    ]
    stores[0].start()

    halo1.wait_recv()
    inside = (seq > 0).astype(F32)
    mixed_ref[:, :, high] = total[:, 0:CH, high].astype(BF)
    for b in range(BATCH):
        prior = (h1r[b].astype(F32) * inside).astype(BF)
        edge1 = tn(prior, hot((16, BLK), lambda r, c: (r == 1) & (c == 0)))
        edge2 = tn(prior, hot((16, BLK), lambda r, c: (r < 2) & (r == c)))
        value = total[b, :, 0:BLK] + (kcol[:, 1:2] * edge1 + kcol[:, 2:3] * edge2)
        mixed_ref[b, :, 0:BLK] = value[0:CH].astype(BF)
    stores[1].start()

    pair.wait_recv()
    fgrad_ref[0] = (fgo[chan] + fgp[half]) + fgr[...].astype(F32)
    stores[2].start()
    arrive(bgr, CHAN, BG)
    bgr[chan] = jnp.zeros((2, 32, BLK), BF)
    got = [bgr[i].astype(F32) for i in range(CHAN)]
    bgrad_ref[...] = bgo[chan] + ((got[0] + got[1]) + (got[2] + got[3]))
    stores[3].start()
    arrive(klr, NL, KL)
    whole = sum((klr[i] for i in range(1, NL)), klr[0])
    kgrad_ref[...] = whole[0:3, 0:CH]
    stores[4].start()

    halo0.wait_send()
    halo1.wait_send()
    for b in range(BATCH):
        for send, sem in ((a0s, A0), (a1s, A1), (a2s, A2), (a3s, A3)):
            sent(send.at[b], NX, sem + b)
        for send, sem in ((b0s, B0), (b1s, B1), (b2s, B2), (b3s, B3)):
            sent(send.at[b], NL, sem + b)
    pltpu.make_async_copy(fgp, fgp, ssem.at[FG]).wait()
    pair.wait_send()
    sent(bgs, CHAN, BG)
    sent(kxr, NX, KX)
    sent(klr, NL, KL)
    for store in stores:
        store.wait()


def emit(*refs):
    ins, outs, held, sem = refs[0:5], refs[5:10], refs[10:15], refs[15]
    parts = [(0, 0), (1, 0), (0, 1), (1, 1), (4, 0), (3, 0), (2, 0)]

    def piece(ref, i, b):
        return ref.at[b] if i < 2 else ref

    loads, stores = [], []
    for n, (i, b) in enumerate(parts):
        source, stage, target = piece(ins[i], i, b), piece(held[i], i, b), piece(outs[i], i, b)
        loads.append(pltpu.make_async_copy(source, stage, sem.at[0, n]))
        stores.append(pltpu.make_async_copy(stage, target, sem.at[1, n]))
    for load in loads:
        load.start()
    for load, store in zip(loads, stores):
        load.wait()
        store.start()
    for store in stores:
        store.wait()


def shards(inputs, first_blocks, second_blocks, kernel, cotangent):
    free = pl.BlockSpec(memory_space=pl.ANY)
    xbuf = pltpu.VMEM((BATCH, NX, 32, ROWS), BF)
    lbuf = pltpu.VMEM((BATCH, NL, 16, ROWS), BF)
    halo = pltpu.VMEM((BATCH, 16, ROWS), BF)
    plane = pltpu.VMEM((BATCH, ROWS, EXT), BF)
    square = pltpu.VMEM((256, 256), BF)
    shapes = (
        jax.ShapeDtypeStruct((BATCH, CH, EXT), BF),
        jax.ShapeDtypeStruct((BATCH, CH, EXT), BF),
        jax.ShapeDtypeStruct((3, CH), F32),
        jax.ShapeDtypeStruct((2, BLK // CHAN, BLK), F32),
        jax.ShapeDtypeStruct((1, 256 // CHAN, 256), F32),
    )
    results = pl.pallas_call(
        body,
        out_shape=shapes,
        in_specs=[free] * 5,
        out_specs=(free,) * 5,
        scratch_shapes=[pltpu.VMEM(one.shape, one.dtype) for one in shapes]
        + [
            plane, plane,
            pltpu.VMEM((2, BLK, BLK), BF), pltpu.VMEM((1, 256, 256), BF),
            pltpu.VMEM((3, CH), F32), plane,
            pltpu.VMEM((BATCH, ROWS, EXT), F32), pltpu.VMEM((BATCH, ROWS, EXT), F32),
            plane, plane, plane,
            pltpu.VMEM((2, BATCH, ROWS, EXT), BF),
            pltpu.VMEM((128, 256), F32), pltpu.VMEM((ROWS, 128), F32),
            square, square, plane,
            pltpu.VMEM((7, 256, 256), BF),
            xbuf, xbuf, lbuf, lbuf, lbuf, lbuf, xbuf, xbuf,
            lbuf, lbuf, xbuf, xbuf, xbuf, xbuf, lbuf, lbuf,
            halo, halo, halo, halo,
            pltpu.VMEM((8, 256), F32), pltpu.VMEM((NX, 8, 256), F32),
            pltpu.VMEM((8, 256), F32), pltpu.VMEM((NL, 8, 256), F32),
            pltpu.VMEM((CHAN, 64, 256), F32),
            pltpu.VMEM((2, 64, 256), F32), pltpu.VMEM((64, 256), BF), pltpu.VMEM((64, 256), BF),
            pltpu.VMEM((CHAN, 2, 32, BLK), F32),
            pltpu.VMEM((CHAN, 2, 32, BLK), BF), pltpu.VMEM((CHAN, 2, 32, BLK), BF),
            pltpu.SemaphoreType.DMA((23,)),
            pltpu.SemaphoreType.DMA((23,)),
            pltpu.SemaphoreType.DMA((5,)),
            pltpu.SemaphoreType.DMA((5,)),
        ],
        compiler_params=pltpu.CompilerParams(
            collective_id=0, has_side_effects=True, vmem_limit_bytes=60 * 1024 * 1024
        ),
    )(inputs, first_blocks, second_blocks, kernel, cotangent)
    return pl.pallas_call(
        emit,
        out_shape=shapes,
        in_specs=[free] * 5,
        out_specs=(free,) * 5,
        scratch_shapes=[pltpu.VMEM(one.shape, one.dtype) for one in shapes]
        + [pltpu.SemaphoreType.DMA((2, 7))],
        compiler_params=pltpu.CompilerParams(vmem_limit_bytes=60 * 1024 * 1024),
    )(*results)


def solution(mesh):
    placed = (
        P(None, "chan", "seq"),
        P("seq", None, None),
        P("seq", None, None),
        P(None, "chan"),
        P(None, "chan", "seq"),
    )
    return jax.shard_map(
        shards,
        mesh=mesh,
        in_specs=placed,
        out_specs=(
            P(None, "chan", "seq"),
            P(None, "chan", "seq"),
            P(None, "chan"),
            P("seq", "chan", None),
            P("seq", "chan", None),
        ),
        check_vma=False,
    )
```

```python
import jax
import jax.numpy as jnp
from jax import lax
from jax.experimental import pallas as pl
from jax.experimental.pallas import tpu as pltpu
from jax.sharding import PartitionSpec as P

NX, NL = 8, 16
SEQ, CHAN = NX * NL, 4
BATCH, CH, EXT, BLK = 2, 240, 256, 128
ROWS = 256
MESH = pl.DeviceIdType.MESH
BF, F32 = jnp.bfloat16, jnp.float32
A0, B0, B1, A1, B2, A2, A3, B3 = range(0, 16, 2)
FG, FH, BG, KX, KL, H0, H1 = range(16, 23)


def dot(a, b, ca, cb):
    return lax.dot_general(a, b, (((ca,), (cb,)), ((), ())), preferred_element_type=F32)


def nn(a, b):
    return dot(a, b, 1, 0)


def nt(a, b):
    return dot(a, b, 1, 1)


def tn(a, b):
    return dot(a, b, 0, 0)


def hot(shape, where):
    row = lax.broadcasted_iota(jnp.int32, shape, 0)
    col = lax.broadcasted_iota(jnp.int32, shape, 1)
    return jnp.where(where(row, col), 1.0, 0.0).astype(BF)


def place0(r, c):
    return ((r >> 4) & 1) * 128 + (r & 15) * 8 + (r >> 5) == c


def turn0(r, c):
    return ((r >> 1) & 7) * 32 + (r & 1) * 16 + (r >> 4) == c


def place1(r, c):
    return ((r >> 3) & 1) * 128 + (r >> 4) * 8 + (r & 7) == c


def turn1(r, c):
    return ((r >> 1) & 15) * 16 + (r & 1) * 8 + (r >> 5) == c


def order1(r, c):
    return ((r >> 1) & 7) * 32 + (r >> 4) * 2 + (r & 1) == c


def flip(where):
    return lambda r, c: where(c, r)


def body(
    x_in, f_in, s_in, k_in, c_in,
    mixed_out, igrad_out, kgrad_out, bgrad_out, fgrad_out,
    mixed_ref, igrad_ref, kgrad_ref, bgrad_ref, fgrad_ref,
    xs, cs, fs, sec, kin, xt, gate, total, gat, mon, mgrad, near, kpad, kcol, st, s11, mgr, tables,
    a0s, a0r, b0s, b0r, b1s, b1r, a1s, a1r,
    b2s, b2r, a2s, a2r, a3s, a3r, b3s, b3r,
    h0s, h0r, h1s, h1r,
    kxs, kxr, kls, klr, fgo, fgp, fgs, fgr, bgo, bgs, bgr,
    ssem, rsem, isem, osem,
):
    seq = lax.axis_index("seq")
    chan = lax.axis_index("chan")
    mx = lax.rem(seq, NX)
    ml = lax.div(seq, NX)
    ahead = lax.rem(seq + 1, SEQ)
    behind = lax.rem(seq + SEQ - 1, SEQ)

    def x_peer(d):
        other = lax.rem(mx + d, NX)
        return other, (ml * NX + other, chan)

    def l_peer(d):
        other = lax.rem(ml + d, NL)
        return other, (other * NX + mx, chan)

    def c_peer(d):
        other = lax.rem(chan + d, CHAN)
        return other, (seq, other)

    barrier = pltpu.get_barrier_semaphore()

    def greet(peer, count):
        def step(d, carry):
            pl.semaphore_signal(barrier, inc=1, device_id=peer(d)[1], device_id_type=MESH)
            return carry

        lax.fori_loop(1, count, step, 0)

    loads = [
        pltpu.make_async_copy(c_in, cs.at[:, pl.ds(0, CH), :], isem.at[2]),
        pltpu.make_async_copy(x_in, xs.at[:, pl.ds(0, CH), :], isem.at[0]),
        pltpu.make_async_copy(f_in, fs, isem.at[1]),
        pltpu.make_async_copy(k_in, kin, isem.at[3]),
        pltpu.make_async_copy(s_in, sec, isem.at[4]),
    ]
    for load in loads:
        load.start()
    greet(l_peer, NL)
    greet(x_peer, NX)
    greet(c_peer, CHAN)
    pl.semaphore_signal(barrier, inc=1, device_id=(ahead, chan), device_id_type=MESH)
    pl.semaphore_signal(barrier, inc=1, device_id=(behind, chan), device_id_type=MESH)

    def remote(src, dst, device, sem):
        return pltpu.make_async_remote_copy(
            src_ref=src, dst_ref=dst, send_sem=ssem.at[sem], recv_sem=rsem.at[sem],
            device_id=device, device_id_type=MESH,
        )

    def scatter(send, recv, mine, peer, count, sem):
        def step(i, carry):
            d = count // 2 + lax.div(i + 1, 2) * (2 * lax.rem(i, 2) - 1)
            other, device = peer(d)
            remote(send.at[other], recv.at[mine], device, sem).start()
            return carry

        lax.fori_loop(0, count - 1, step, 0)

    def keep(send, recv, mine):
        recv[mine] = send[mine]

    def spread(send, recv, mine, peer, count, sem):
        def step(i, carry):
            d = count // 2 + lax.div(i + 1, 2) * (2 * lax.rem(i, 2) - 1)
            remote(send, recv.at[mine], peer(d)[1], sem).start()
            return carry

        lax.fori_loop(0, count - 1, step, 0)
        recv[mine] = send[...]

    def arrive(recv, count, sem):
        part = recv.at[pl.ds(0, count - 1)]
        pltpu.make_async_copy(part, part, rsem.at[sem]).wait()

    def sent(send, count, sem):
        part = send.at[pl.ds(0, count - 1)]
        pltpu.make_async_copy(part, part, ssem.at[sem]).wait()

    def flat(ref, b):
        return ref[b].reshape(256, ROWS)

    def over_x(value, send, recv, b, sem):
        send[b] = value.astype(BF).reshape(NX, 32, ROWS)
        scatter(send.at[b], recv.at[b], mx, x_peer, NX, sem + b)
        keep(send.at[b], recv.at[b], mx)

    def over_l(value, send, recv, b, sem):
        send[b] = value.astype(BF).reshape(NL, 16, ROWS)
        scatter(send.at[b], recv.at[b], ml, l_peer, NL, sem + b)
        keep(send.at[b], recv.at[b], ml)

    zero_rows = jnp.zeros((BATCH, ROWS - CH, EXT), BF)
    xs[:, CH:ROWS, :] = zero_rows
    cs[:, CH:ROWS, :] = zero_rows
    kpad[...] = jnp.zeros_like(kpad)
    tables[0] = hot((256, 256), place0)
    tables[1] = hot((256, 256), place1)
    shift1 = hot((EXT, EXT), lambda r, c: r == c + 1)
    shift2 = hot((EXT, EXT), lambda r, c: r == c + 2)

    loads[0].wait()
    head = hot((16, EXT), lambda r, c: (r == c) & (r < 2))
    for b in range(BATCH):
        h0s[b] = nt(head, cs[b]).astype(BF)
    loads[1].wait()
    loads[2].wait()
    p0 = tables[0]
    for b in range(BATCH):
        m0 = nn(xs[b, :, 0:BLK], fs[0]).astype(BF)
        m1 = nn(xs[b, :, BLK:EXT], fs[1]).astype(BF)
        rows = nt(p0[:, 0:BLK], m0) + nt(p0[:, BLK:EXT], m1)
        a0s[b] = rows.astype(BF).reshape(NX, 32, ROWS)

    loads[3].wait()
    kpad[0:3, 0:CH] = kin[...]
    kcol[0:128, :] = kpad[:, 0:128].T
    kcol[128:256, :] = kpad[:, 128:256].T

    def gate_from(lanes, b, cot, near1, near2):
        near[0, b, :, lanes] = near1.astype(BF)
        near[1, b, :, lanes] = near2.astype(BF)
        value = kcol[:, 0:1] * cot.astype(F32) + kcol[:, 1:2] * near1 + kcol[:, 2:3] * near2
        gate[b, :, lanes] = value
        mgrad[b, :, lanes] = (value * xs[b, :, lanes].astype(F32)).astype(BF)

    last = NL - 1
    p1 = tables[1]
    for b in range(BATCH):
        gate_from(slice(0, EXT), b, cs[b], nn(cs[b], shift1), nn(cs[b], shift2))
        b1s[b] = nt(p1, mgrad[b]).astype(BF).reshape(NL, 16, ROWS)

    pl.semaphore_wait(barrier, NX - 1 + NL - 1 + CHAN - 1 + 2)

    halo0 = remote(h0s, h0r, (behind, chan), H0)
    halo0.start()
    for b in range(BATCH):
        scatter(a0s.at[b], a0r.at[b], mx, x_peer, NX, A0 + b)
    for b in range(BATCH):

        def step(i, carry):
            other, device = l_peer(NL // 2 + lax.div(i + 1, 2) * (2 * lax.rem(i, 2) - 1))

            @pl.when(other != last)
            def _():
                remote(b1s.at[b, other], b1r.at[b, ml], device, B1 + b).start()

            return carry

        lax.fori_loop(0, NL - 1, step, 0)
    for b in range(BATCH):
        keep(a0s.at[b], a0r.at[b], mx)

    tables[2] = hot((256, 256), turn0)
    tables[3] = hot((256, 256), flip(turn0))
    tables[4] = hot((256, 256), turn1)
    tables[5] = hot((256, 256), flip(turn1))
    tables[6] = hot((256, 256), order1)
    loads[4].wait()
    eye = hot((256, 256), lambda r, c: r == c)
    second = sec[0]
    st[...] = nt(eye, second).astype(BF)
    back = hot((256, 256), flip(order1))
    s11[...] = nt(nn(back, second).astype(BF), back).astype(BF)

    arrive(a0r.at[0], NX, A0)
    over_l(nn(tables[2], flat(a0r, 0)), b0s, b0r, 0, B0)

    halo0.wait_recv()
    inside = (seq < SEQ - 1).astype(F32)
    high = slice(BLK, EXT)
    for b in range(BATCH):
        tail = (h0r[b].astype(F32) * inside).astype(BF)
        near1 = near[0, b, :, high].astype(F32)
        near2 = near[1, b, :, high].astype(F32)
        near1 = near1 + tn(tail, hot((16, BLK), lambda r, c: (r == 0) & (c == BLK - 1)))
        near2 = near2 + tn(tail, hot((16, BLK), lambda r, c: (r < 2) & (c == BLK - 2 + r)))
        gate_from(high, b, cs[b, :, high], near1, near2)
        b1s[b, last] = nt(tables[1, 16 * last : 16 * NL], mgrad[b]).astype(BF)

        @pl.when(ml != last)
        def _():
            remote(b1s.at[b, last], b1r.at[b, ml], (last * NX + mx, chan), B1 + b).start()

        keep(b1s.at[b], b1r.at[b], ml)

    arrive(a0r.at[1], NX, A0 + 1)
    over_l(nn(tables[2], flat(a0r, 1)), b0s, b0r, 1, B0)

    for b in range(BATCH):
        xt[b] = nt(eye, xs[b]).astype(BF)
    for b in range(BATCH):
        arrive(b1r.at[b], NL, B1 + b)
        over_x(nn(tables[4], flat(b1r, b)), a1s, a1r, b, A1)
    for b in range(BATCH):
        arrive(b0r.at[b], NL, B0 + b)
        over_l(nn(st[...], flat(b0r, b)), b2s, b2r, b, B2)
    for b in range(BATCH):
        arrive(a1r.at[b], NX, A1 + b)
        over_x(nn(s11[...], flat(a1r, b)), a3s, a3r, b, A3)
    grad = jnp.zeros((256, 256), F32)
    for b in range(BATCH):
        nat = nn(tables[6], flat(a1r, b)).astype(BF)
        grad = grad + nt(flat(b0r, b), nat)
    fgo[...] = grad.reshape(CHAN, 64, 256)
    core = lax.rem(chan, 2)
    half = lax.div(chan, 2)
    for h in range(2):
        remote(fgo.at[2 * h + 1 - core], fgp.at[h], (seq, 2 * half + 1 - core), FG).start()
    for b in range(BATCH):
        arrive(b2r.at[b], NL, B2 + b)
        over_x(nn(tables[3], flat(b2r, b)), a2s, a2r, b, A2)
        arrive(a3r.at[b], NX, A3 + b)
        over_l(nn(tables[5], flat(a3r, b)), b3s, b3r, b, B3)

    prods = [jnp.zeros((ROWS, BLK), F32)] * 3
    for b in range(BATCH):
        arrive(a2r.at[b], NX, A2 + b)
        monarch = tn(flat(a2r, b), tables[0])
        mon[b] = monarch.astype(BF)
        gated = (xs[b].astype(F32) * monarch).astype(BF)
        gat[b] = gated
        gated32 = gated.astype(F32)
        for j in range(3):
            window = cs[b] if j == 0 else near[j - 1, b]
            prod = gated32 * window.astype(F32)
            prods[j] = prods[j] + (prod[:, 0:BLK] + prod[:, BLK:EXT])
    sums = [jnp.sum(prod, axis=1, keepdims=True) for prod in prods]
    lane = lax.broadcasted_iota(jnp.int32, (128, 128), 1)
    wide = jnp.zeros((128, 128), F32)
    for j in range(3):
        wide = jnp.where(lane == j, sums[j][0:128], jnp.where(lane == 3 + j, sums[j][128:256], wide))
    kxs[...] = wide.T[0:8]
    spread(kxs, kxr, mx, x_peer, NX, KX)

    edge = hot((16, EXT), lambda r, c: (r < 2) & (c == EXT - 2 + r))
    for b in range(BATCH):
        h1s[b] = nt(edge, gat[b]).astype(BF)
    halo1 = remote(h1s, h1r, (ahead, chan), H1)
    halo1.start()
    pltpu.make_async_copy(fgp, fgp, rsem.at[FG]).wait()
    fgs[...] = (fgo[2 * (1 - half) + core] + fgp[1 - half]).astype(BF)
    pair = remote(fgs, fgr, (seq, 2 * (1 - half) + core), FH)
    pair.start()

    for b in range(BATCH):
        arrive(b3r.at[b], NL, B3 + b)
        mgr[b] = tn(flat(b3r, b), tables[1]).astype(BF)
    for q in range(2):
        lanes = slice(q * BLK, (q + 1) * BLK)
        part = nn(xt[0, lanes, :], mgr[0, :, lanes]) + nn(xt[1, lanes, :], mgr[1, :, lanes])
        part = part.reshape(CHAN, 32, BLK)
        for o in range(CHAN):
            bgo[o, q] = part[o]
            bgs[o, q] = part[o].astype(BF)
    scatter(bgs, bgr, chan, c_peer, CHAN, BG)

    arrive(kxr, NX, KX)
    kls[...] = sum((kxr[i] for i in range(1, NX)), kxr[0])
    spread(kls, klr, ml, l_peer, NL, KL)

    far1 = hot((EXT, EXT), lambda r, c: r + 1 == c)
    far2 = hot((EXT, EXT), lambda r, c: r + 2 == c)
    for b in range(BATCH):
        total[b] = (
            kcol[:, 0:1] * gat[b].astype(F32)
            + kcol[:, 1:2] * nn(gat[b], far1)
            + kcol[:, 2:3] * nn(gat[b], far2)
        )
    for q in range(2):
        lanes = slice(q * BLK, (q + 1) * BLK)
        for b in range(BATCH):
            through = nt(mgr[b, :, lanes], fs[q])
            direct = gate[b, :, lanes] * mon[b, :, lanes].astype(F32)
            igrad_ref[b, :, lanes] = (direct + through)[0:CH].astype(BF)

    stores = [
        pltpu.make_async_copy(igrad_ref, igrad_out, osem.at[0]),
        pltpu.make_async_copy(mixed_ref, mixed_out, osem.at[1]),
        pltpu.make_async_copy(fgrad_ref, fgrad_out, osem.at[2]),
        pltpu.make_async_copy(bgrad_ref, bgrad_out, osem.at[3]),
        pltpu.make_async_copy(kgrad_ref, kgrad_out, osem.at[4]),
    ]
    stores[0].start()

    halo1.wait_recv()
    inside = (seq > 0).astype(F32)
    mixed_ref[:, :, high] = total[:, 0:CH, high].astype(BF)
    for b in range(BATCH):
        prior = (h1r[b].astype(F32) * inside).astype(BF)
        edge1 = tn(prior, hot((16, BLK), lambda r, c: (r == 1) & (c == 0)))
        edge2 = tn(prior, hot((16, BLK), lambda r, c: (r < 2) & (r == c)))
        value = total[b, :, 0:BLK] + (kcol[:, 1:2] * edge1 + kcol[:, 2:3] * edge2)
        mixed_ref[b, :, 0:BLK] = value[0:CH].astype(BF)
    stores[1].start()

    pair.wait_recv()
    fgrad_ref[0] = (fgo[chan] + fgp[half]) + fgr[...].astype(F32)
    stores[2].start()
    arrive(bgr, CHAN, BG)
    bgr[chan] = jnp.zeros((2, 32, BLK), BF)
    got = [bgr[i].astype(F32) for i in range(CHAN)]
    bgrad_ref[...] = bgo[chan] + ((got[0] + got[1]) + (got[2] + got[3]))
    stores[3].start()
    arrive(klr, NL, KL)
    whole = sum((klr[i] for i in range(1, NL)), klr[0])
    kgrad_ref[:, 0:128] = whole[0:3]
    kgrad_ref[:, 128:CH] = whole[3:6, 0 : CH - 128]
    stores[4].start()

    halo0.wait_send()
    halo1.wait_send()
    for b in range(BATCH):
        for send, sem in ((a0s, A0), (a1s, A1), (a2s, A2), (a3s, A3)):
            sent(send.at[b], NX, sem + b)
        for send, sem in ((b0s, B0), (b1s, B1), (b2s, B2), (b3s, B3)):
            sent(send.at[b], NL, sem + b)
    pltpu.make_async_copy(fgp, fgp, ssem.at[FG]).wait()
    pair.wait_send()
    sent(bgs, CHAN, BG)
    sent(kxr, NX, KX)
    sent(klr, NL, KL)
    for store in stores:
        store.wait()


def emit(*refs):
    ins, outs, held, sem = refs[0:5], refs[5:10], refs[10:15], refs[15]
    parts = [(0, 0), (1, 0), (0, 1), (1, 1), (4, 0), (3, 0), (2, 0)]

    def piece(ref, i, b):
        return ref.at[b] if i < 2 else ref

    loads, stores = [], []
    for n, (i, b) in enumerate(parts):
        source, stage, target = piece(ins[i], i, b), piece(held[i], i, b), piece(outs[i], i, b)
        loads.append(pltpu.make_async_copy(source, stage, sem.at[0, n]))
        stores.append(pltpu.make_async_copy(stage, target, sem.at[1, n]))
    for load in loads:
        load.start()
    for load, store in zip(loads, stores):
        load.wait()
        store.start()
    for store in stores:
        store.wait()


def shards(inputs, first_blocks, second_blocks, kernel, cotangent):
    free = pl.BlockSpec(memory_space=pl.ANY)
    xbuf = pltpu.VMEM((BATCH, NX, 32, ROWS), BF)
    lbuf = pltpu.VMEM((BATCH, NL, 16, ROWS), BF)
    halo = pltpu.VMEM((BATCH, 16, ROWS), BF)
    plane = pltpu.VMEM((BATCH, ROWS, EXT), BF)
    square = pltpu.VMEM((256, 256), BF)
    shapes = (
        jax.ShapeDtypeStruct((BATCH, CH, EXT), BF),
        jax.ShapeDtypeStruct((BATCH, CH, EXT), BF),
        jax.ShapeDtypeStruct((3, CH), F32),
        jax.ShapeDtypeStruct((2, BLK // CHAN, BLK), F32),
        jax.ShapeDtypeStruct((1, 256 // CHAN, 256), F32),
    )
    results = pl.pallas_call(
        body,
        out_shape=shapes,
        in_specs=[free] * 5,
        out_specs=(free,) * 5,
        scratch_shapes=[pltpu.VMEM(one.shape, one.dtype) for one in shapes]
        + [
            plane, plane,
            pltpu.VMEM((2, BLK, BLK), BF), pltpu.VMEM((1, 256, 256), BF),
            pltpu.VMEM((3, CH), F32), plane,
            pltpu.VMEM((BATCH, ROWS, EXT), F32), pltpu.VMEM((BATCH, ROWS, EXT), F32),
            plane, plane, plane,
            pltpu.VMEM((2, BATCH, ROWS, EXT), BF),
            pltpu.VMEM((128, 256), F32), pltpu.VMEM((ROWS, 128), F32),
            square, square, plane,
            pltpu.VMEM((7, 256, 256), BF),
            xbuf, xbuf, lbuf, lbuf, lbuf, lbuf, xbuf, xbuf,
            lbuf, lbuf, xbuf, xbuf, xbuf, xbuf, lbuf, lbuf,
            halo, halo, halo, halo,
            pltpu.VMEM((8, 128), F32), pltpu.VMEM((NX, 8, 128), F32),
            pltpu.VMEM((8, 128), F32), pltpu.VMEM((NL, 8, 128), F32),
            pltpu.VMEM((CHAN, 64, 256), F32),
            pltpu.VMEM((2, 64, 256), F32), pltpu.VMEM((64, 256), BF), pltpu.VMEM((64, 256), BF),
            pltpu.VMEM((CHAN, 2, 32, BLK), F32),
            pltpu.VMEM((CHAN, 2, 32, BLK), BF), pltpu.VMEM((CHAN, 2, 32, BLK), BF),
            pltpu.SemaphoreType.DMA((23,)),
            pltpu.SemaphoreType.DMA((23,)),
            pltpu.SemaphoreType.DMA((5,)),
            pltpu.SemaphoreType.DMA((5,)),
        ],
        compiler_params=pltpu.CompilerParams(
            collective_id=0, has_side_effects=True, vmem_limit_bytes=60 * 1024 * 1024
        ),
    )(inputs, first_blocks, second_blocks, kernel, cotangent)
    return pl.pallas_call(
        emit,
        out_shape=shapes,
        in_specs=[free] * 5,
        out_specs=(free,) * 5,
        scratch_shapes=[pltpu.VMEM(one.shape, one.dtype) for one in shapes]
        + [pltpu.SemaphoreType.DMA((2, 7))],
        compiler_params=pltpu.CompilerParams(vmem_limit_bytes=60 * 1024 * 1024),
    )(*results)


def solution(mesh):
    placed = (
        P(None, "chan", "seq"),
        P("seq", None, None),
        P("seq", None, None),
        P(None, "chan"),
        P(None, "chan", "seq"),
    )
    return jax.shard_map(
        shards,
        mesh=mesh,
        in_specs=placed,
        out_specs=(
            P(None, "chan", "seq"),
            P(None, "chan", "seq"),
            P(None, "chan"),
            P("seq", "chan", None),
            P("seq", "chan", None),
        ),
        check_vma=False,
    )
```

```python
import jax
import jax.numpy as jnp
from jax import lax
from jax.experimental import pallas as pl
from jax.experimental.pallas import tpu as pltpu
from jax.sharding import PartitionSpec as P

NX, NL = 8, 16
SEQ, CHAN = NX * NL, 4
BATCH, CH, EXT, BLK = 2, 240, 256, 128
ROWS = 256
MESH = pl.DeviceIdType.MESH
BF, F32 = jnp.bfloat16, jnp.float32
A0, B0, B1, A1, B2, A2, A3, B3 = range(0, 16, 2)
FG, FH, BG, KX, KL, H0, H1 = range(16, 23)


def dot(a, b, ca, cb):
    return lax.dot_general(a, b, (((ca,), (cb,)), ((), ())), preferred_element_type=F32)


def nn(a, b):
    return dot(a, b, 1, 0)


def nt(a, b):
    return dot(a, b, 1, 1)


def tn(a, b):
    return dot(a, b, 0, 0)


def hot(shape, where):
    row = lax.broadcasted_iota(jnp.int32, shape, 0)
    col = lax.broadcasted_iota(jnp.int32, shape, 1)
    return jnp.where(where(row, col), 1.0, 0.0).astype(BF)


def place0(r, c):
    return ((r >> 4) & 1) * 128 + (r & 15) * 8 + (r >> 5) == c


def turn0(r, c):
    return ((r >> 1) & 7) * 32 + (r & 1) * 16 + (r >> 4) == c


def place1(r, c):
    return ((r >> 3) & 1) * 128 + (r >> 4) * 8 + (r & 7) == c


def turn1(r, c):
    return ((r >> 1) & 15) * 16 + (r & 1) * 8 + (r >> 5) == c


def order1(r, c):
    return ((r >> 1) & 7) * 32 + (r >> 4) * 2 + (r & 1) == c


def flip(where):
    return lambda r, c: where(c, r)


def body(
    x_in, f_in, s_in, k_in, c_in,
    mixed_out, igrad_out, kgrad_out, bgrad_out, fgrad_out,
    mixed_ref, igrad_ref, kgrad_ref, bgrad_ref, fgrad_ref,
    xs, cs, fs, sec, kin, xt, gate, total, gat, mon, mgrad, near, kpad, kcol, st, s11, mgr, tables,
    a0s, a0r, b0s, b0r, b1s, b1r, a1s, a1r,
    b2s, b2r, a2s, a2r, a3s, a3r, b3s, b3r,
    h0s, h0r, h1s, h1r,
    kxs, kxr, kls, klr, fgo, fgp, fgs, fgr, bgo, bgs, bgr,
    ssem, rsem, isem, osem,
):
    seq = lax.axis_index("seq")
    chan = lax.axis_index("chan")
    mx = lax.rem(seq, NX)
    ml = lax.div(seq, NX)
    ahead = lax.rem(seq + 1, SEQ)
    behind = lax.rem(seq + SEQ - 1, SEQ)

    def x_peer(d):
        other = lax.rem(mx + d, NX)
        return other, (ml * NX + other, chan)

    def l_peer(d):
        other = lax.rem(ml + d, NL)
        return other, (other * NX + mx, chan)

    def c_peer(d):
        other = lax.rem(chan + d, CHAN)
        return other, (seq, other)

    barrier = pltpu.get_barrier_semaphore()

    def greet(peer, count):
        def step(d, carry):
            pl.semaphore_signal(barrier, inc=1, device_id=peer(d)[1], device_id_type=MESH)
            return carry

        lax.fori_loop(1, count, step, 0)

    loads = [
        pltpu.make_async_copy(c_in, cs.at[:, pl.ds(0, CH), :], isem.at[2]),
        pltpu.make_async_copy(x_in, xs.at[:, pl.ds(0, CH), :], isem.at[0]),
        pltpu.make_async_copy(f_in, fs, isem.at[1]),
        pltpu.make_async_copy(k_in, kin, isem.at[3]),
        pltpu.make_async_copy(s_in, sec, isem.at[4]),
    ]
    for load in loads:
        load.start()
    greet(l_peer, NL)
    greet(x_peer, NX)
    greet(c_peer, CHAN)
    pl.semaphore_signal(barrier, inc=1, device_id=(ahead, chan), device_id_type=MESH)
    pl.semaphore_signal(barrier, inc=1, device_id=(behind, chan), device_id_type=MESH)

    def remote(src, dst, device, sem):
        return pltpu.make_async_remote_copy(
            src_ref=src, dst_ref=dst, send_sem=ssem.at[sem], recv_sem=rsem.at[sem],
            device_id=device, device_id_type=MESH,
        )

    def scatter(send, recv, mine, peer, count, sem):
        def step(i, carry):
            d = count // 2 + lax.div(i + 1, 2) * (2 * lax.rem(i, 2) - 1)
            other, device = peer(d)
            remote(send.at[other], recv.at[mine], device, sem).start()
            return carry

        lax.fori_loop(0, count - 1, step, 0)

    def keep(send, recv, mine):
        recv[mine] = send[mine]

    def spread(send, recv, mine, peer, count, sem):
        def step(i, carry):
            d = count // 2 + lax.div(i + 1, 2) * (2 * lax.rem(i, 2) - 1)
            remote(send, recv.at[mine], peer(d)[1], sem).start()
            return carry

        lax.fori_loop(0, count - 1, step, 0)
        recv[mine] = send[...]

    def arrive(recv, count, sem):
        part = recv.at[pl.ds(0, count - 1)]
        pltpu.make_async_copy(part, part, rsem.at[sem]).wait()

    def sent(send, count, sem):
        part = send.at[pl.ds(0, count - 1)]
        pltpu.make_async_copy(part, part, ssem.at[sem]).wait()

    def flat(ref, b):
        return ref[b].reshape(256, ROWS)

    def over_x(value, send, recv, b, sem):
        send[b] = value.astype(BF).reshape(NX, 32, ROWS)
        scatter(send.at[b], recv.at[b], mx, x_peer, NX, sem + b)
        keep(send.at[b], recv.at[b], mx)

    def over_l(value, send, recv, b, sem):
        send[b] = value.astype(BF).reshape(NL, 16, ROWS)
        scatter(send.at[b], recv.at[b], ml, l_peer, NL, sem + b)
        keep(send.at[b], recv.at[b], ml)

    zero_rows = jnp.zeros((BATCH, ROWS - CH, EXT), BF)
    xs[:, CH:ROWS, :] = zero_rows
    cs[:, CH:ROWS, :] = zero_rows
    kpad[...] = jnp.zeros_like(kpad)
    tables[0] = hot((256, 256), place0)
    tables[1] = hot((256, 256), place1)
    shift1 = hot((EXT, EXT), lambda r, c: r == c + 1)
    shift2 = hot((EXT, EXT), lambda r, c: r == c + 2)

    loads[0].wait()
    head = hot((16, EXT), lambda r, c: (r == c) & (r < 2))
    for b in range(BATCH):
        h0s[b] = nt(head, cs[b]).astype(BF)
    loads[1].wait()
    loads[2].wait()
    p0 = tables[0]
    for b in range(BATCH):
        m0 = nn(xs[b, :, 0:BLK], fs[0]).astype(BF)
        m1 = nn(xs[b, :, BLK:EXT], fs[1]).astype(BF)
        rows = nt(p0[:, 0:BLK], m0) + nt(p0[:, BLK:EXT], m1)
        a0s[b] = rows.astype(BF).reshape(NX, 32, ROWS)

    loads[3].wait()
    kpad[0:3, 0:CH] = kin[...]
    kcol[0:128, :] = kpad[:, 0:128].T
    kcol[128:256, :] = kpad[:, 128:256].T

    def gate_from(lanes, b, cot, near1, near2):
        near[0, b, :, lanes] = near1.astype(BF)
        near[1, b, :, lanes] = near2.astype(BF)
        value = kcol[:, 0:1] * cot.astype(F32) + kcol[:, 1:2] * near1 + kcol[:, 2:3] * near2
        gate[b, :, lanes] = value
        mgrad[b, :, lanes] = (value * xs[b, :, lanes].astype(F32)).astype(BF)

    last = NL - 1
    p1 = tables[1]
    for b in range(BATCH):
        gate_from(slice(0, EXT), b, cs[b], nn(cs[b], shift1), nn(cs[b], shift2))
        b1s[b] = nt(p1, mgrad[b]).astype(BF).reshape(NL, 16, ROWS)

    pl.semaphore_wait(barrier, NX - 1 + NL - 1 + CHAN - 1 + 2)

    halo0 = remote(h0s, h0r, (behind, chan), H0)
    halo0.start()
    for b in range(BATCH):
        scatter(a0s.at[b], a0r.at[b], mx, x_peer, NX, A0 + b)
    for b in range(BATCH):

        def step(i, carry):
            other, device = l_peer(NL // 2 + lax.div(i + 1, 2) * (2 * lax.rem(i, 2) - 1))

            @pl.when(other != last)
            def _():
                remote(b1s.at[b, other], b1r.at[b, ml], device, B1 + b).start()

            return carry

        lax.fori_loop(0, NL - 1, step, 0)
    for b in range(BATCH):
        keep(a0s.at[b], a0r.at[b], mx)

    tables[2] = hot((256, 256), turn0)
    tables[3] = hot((256, 256), flip(turn0))
    tables[4] = hot((256, 256), turn1)
    tables[5] = hot((256, 256), flip(turn1))
    tables[6] = hot((256, 256), order1)
    loads[4].wait()
    eye = hot((256, 256), lambda r, c: r == c)
    second = sec[0]
    st[...] = nt(eye, second).astype(BF)
    back = hot((256, 256), flip(order1))
    s11[...] = nt(nn(back, second).astype(BF), back).astype(BF)

    arrive(a0r.at[0], NX, A0)
    over_l(nn(tables[2], flat(a0r, 0)), b0s, b0r, 0, B0)

    halo0.wait_recv()
    inside = (seq < SEQ - 1).astype(F32)
    high = slice(BLK, EXT)
    for b in range(BATCH):
        tail = (h0r[b].astype(F32) * inside).astype(BF)
        near1 = near[0, b, :, high].astype(F32)
        near2 = near[1, b, :, high].astype(F32)
        near1 = near1 + tn(tail, hot((16, BLK), lambda r, c: (r == 0) & (c == BLK - 1)))
        near2 = near2 + tn(tail, hot((16, BLK), lambda r, c: (r < 2) & (c == BLK - 2 + r)))
        gate_from(high, b, cs[b, :, high], near1, near2)
        b1s[b, last] = nt(tables[1, 16 * last : 16 * NL], mgrad[b]).astype(BF)

        @pl.when(ml != last)
        def _():
            remote(b1s.at[b, last], b1r.at[b, ml], (last * NX + mx, chan), B1 + b).start()

        keep(b1s.at[b], b1r.at[b], ml)

    arrive(a0r.at[1], NX, A0 + 1)
    over_l(nn(tables[2], flat(a0r, 1)), b0s, b0r, 1, B0)

    for b in range(BATCH):
        xt[b] = nt(eye, xs[b]).astype(BF)
    for b in range(BATCH):
        arrive(b1r.at[b], NL, B1 + b)
        over_x(nn(tables[4], flat(b1r, b)), a1s, a1r, b, A1)
    for b in range(BATCH):
        arrive(b0r.at[b], NL, B0 + b)
        over_l(nn(st[...], flat(b0r, b)), b2s, b2r, b, B2)
    for b in range(BATCH):
        arrive(a1r.at[b], NX, A1 + b)
        over_x(nn(s11[...], flat(a1r, b)), a3s, a3r, b, A3)
    for b in range(BATCH):
        arrive(b2r.at[b], NL, B2 + b)
        over_x(nn(tables[3], flat(b2r, b)), a2s, a2r, b, A2)
        arrive(a3r.at[b], NX, A3 + b)
        over_l(nn(tables[5], flat(a3r, b)), b3s, b3r, b, B3)

    grad = jnp.zeros((256, 256), F32)
    for b in range(BATCH):
        nat = nn(tables[6], flat(a1r, b)).astype(BF)
        grad = grad + nt(flat(b0r, b), nat)
    fgo[...] = grad.reshape(CHAN, 64, 256)
    core = lax.rem(chan, 2)
    half = lax.div(chan, 2)
    for h in range(2):
        remote(fgo.at[2 * h + 1 - core], fgp.at[h], (seq, 2 * half + 1 - core), FG).start()

    prods = [jnp.zeros((ROWS, BLK), F32)] * 3
    for b in range(BATCH):
        arrive(a2r.at[b], NX, A2 + b)
        monarch = tn(flat(a2r, b), tables[0])
        mon[b] = monarch.astype(BF)
        gated = (xs[b].astype(F32) * monarch).astype(BF)
        gat[b] = gated
        gated32 = gated.astype(F32)
        for j in range(3):
            window = cs[b] if j == 0 else near[j - 1, b]
            prod = gated32 * window.astype(F32)
            prods[j] = prods[j] + (prod[:, 0:BLK] + prod[:, BLK:EXT])
    sums = [jnp.sum(prod, axis=1, keepdims=True) for prod in prods]
    lane = lax.broadcasted_iota(jnp.int32, (128, 128), 1)
    wide = jnp.zeros((128, 128), F32)
    for j in range(3):
        wide = jnp.where(lane == j, sums[j][0:128], jnp.where(lane == 3 + j, sums[j][128:256], wide))
    kxs[...] = wide.T[0:8]
    spread(kxs, kxr, mx, x_peer, NX, KX)

    edge = hot((16, EXT), lambda r, c: (r < 2) & (c == EXT - 2 + r))
    for b in range(BATCH):
        h1s[b] = nt(edge, gat[b]).astype(BF)
    halo1 = remote(h1s, h1r, (ahead, chan), H1)
    halo1.start()
    pltpu.make_async_copy(fgp, fgp, rsem.at[FG]).wait()
    fgs[...] = (fgo[2 * (1 - half) + core] + fgp[1 - half]).astype(BF)
    pair = remote(fgs, fgr, (seq, 2 * (1 - half) + core), FH)
    pair.start()

    parts = [jnp.zeros((BLK, BLK), F32)] * 2
    for b in range(BATCH):
        arrive(b3r.at[b], NL, B3 + b)
        mgr[b] = tn(flat(b3r, b), tables[1]).astype(BF)
        for q in range(2):
            lanes = slice(q * BLK, (q + 1) * BLK)
            parts[q] = parts[q] + nn(xt[b, lanes, :], mgr[b, :, lanes])
        if b == 0:
            arrive(kxr, NX, KX)
            kls[...] = sum((kxr[i] for i in range(1, NX)), kxr[0])
            spread(kls, klr, ml, l_peer, NL, KL)
    for q in range(2):
        part = parts[q].reshape(CHAN, 32, BLK)
        for o in range(CHAN):
            bgo[o, q] = part[o]
            bgs[o, q] = part[o].astype(BF)
    scatter(bgs, bgr, chan, c_peer, CHAN, BG)

    far1 = hot((EXT, EXT), lambda r, c: r + 1 == c)
    far2 = hot((EXT, EXT), lambda r, c: r + 2 == c)
    for b in range(BATCH):
        total[b] = (
            kcol[:, 0:1] * gat[b].astype(F32)
            + kcol[:, 1:2] * nn(gat[b], far1)
            + kcol[:, 2:3] * nn(gat[b], far2)
        )
    for q in range(2):
        lanes = slice(q * BLK, (q + 1) * BLK)
        for b in range(BATCH):
            through = nt(mgr[b, :, lanes], fs[q])
            direct = gate[b, :, lanes] * mon[b, :, lanes].astype(F32)
            igrad_ref[b, :, lanes] = (direct + through)[0:CH].astype(BF)

    stores = [
        pltpu.make_async_copy(igrad_ref, igrad_out, osem.at[0]),
        pltpu.make_async_copy(mixed_ref, mixed_out, osem.at[1]),
        pltpu.make_async_copy(fgrad_ref, fgrad_out, osem.at[2]),
        pltpu.make_async_copy(bgrad_ref, bgrad_out, osem.at[3]),
        pltpu.make_async_copy(kgrad_ref, kgrad_out, osem.at[4]),
    ]
    stores[0].start()

    halo1.wait_recv()
    inside = (seq > 0).astype(F32)
    mixed_ref[:, :, high] = total[:, 0:CH, high].astype(BF)
    for b in range(BATCH):
        prior = (h1r[b].astype(F32) * inside).astype(BF)
        edge1 = tn(prior, hot((16, BLK), lambda r, c: (r == 1) & (c == 0)))
        edge2 = tn(prior, hot((16, BLK), lambda r, c: (r < 2) & (r == c)))
        value = total[b, :, 0:BLK] + (kcol[:, 1:2] * edge1 + kcol[:, 2:3] * edge2)
        mixed_ref[b, :, 0:BLK] = value[0:CH].astype(BF)
    stores[1].start()

    pair.wait_recv()
    fgrad_ref[0] = (fgo[chan] + fgp[half]) + fgr[...].astype(F32)
    stores[2].start()
    arrive(bgr, CHAN, BG)
    bgr[chan] = jnp.zeros((2, 32, BLK), BF)
    got = [bgr[i].astype(F32) for i in range(CHAN)]
    bgrad_ref[...] = bgo[chan] + ((got[0] + got[1]) + (got[2] + got[3]))
    stores[3].start()
    arrive(klr, NL, KL)
    whole = sum((klr[i] for i in range(1, NL)), klr[0])
    kgrad_ref[:, 0:128] = whole[0:3]
    kgrad_ref[:, 128:CH] = whole[3:6, 0 : CH - 128]
    stores[4].start()

    halo0.wait_send()
    halo1.wait_send()
    for b in range(BATCH):
        for send, sem in ((a0s, A0), (a1s, A1), (a2s, A2), (a3s, A3)):
            sent(send.at[b], NX, sem + b)
        for send, sem in ((b0s, B0), (b1s, B1), (b2s, B2), (b3s, B3)):
            sent(send.at[b], NL, sem + b)
    pltpu.make_async_copy(fgp, fgp, ssem.at[FG]).wait()
    pair.wait_send()
    sent(bgs, CHAN, BG)
    sent(kxr, NX, KX)
    sent(klr, NL, KL)
    for store in stores:
        store.wait()


def emit(*refs):
    ins, outs, held, sem = refs[0:5], refs[5:10], refs[10:15], refs[15]
    parts = [(0, 0), (1, 0), (0, 1), (1, 1), (4, 0), (3, 0), (2, 0)]

    def piece(ref, i, b):
        return ref.at[b] if i < 2 else ref

    loads, stores = [], []
    for n, (i, b) in enumerate(parts):
        source, stage, target = piece(ins[i], i, b), piece(held[i], i, b), piece(outs[i], i, b)
        loads.append(pltpu.make_async_copy(source, stage, sem.at[0, n]))
        stores.append(pltpu.make_async_copy(stage, target, sem.at[1, n]))
    for load in loads:
        load.start()
    for load, store in zip(loads, stores):
        load.wait()
        store.start()
    for store in stores:
        store.wait()


def shards(inputs, first_blocks, second_blocks, kernel, cotangent):
    free = pl.BlockSpec(memory_space=pl.ANY)
    xbuf = pltpu.VMEM((BATCH, NX, 32, ROWS), BF)
    lbuf = pltpu.VMEM((BATCH, NL, 16, ROWS), BF)
    halo = pltpu.VMEM((BATCH, 16, ROWS), BF)
    plane = pltpu.VMEM((BATCH, ROWS, EXT), BF)
    square = pltpu.VMEM((256, 256), BF)
    shapes = (
        jax.ShapeDtypeStruct((BATCH, CH, EXT), BF),
        jax.ShapeDtypeStruct((BATCH, CH, EXT), BF),
        jax.ShapeDtypeStruct((3, CH), F32),
        jax.ShapeDtypeStruct((2, BLK // CHAN, BLK), F32),
        jax.ShapeDtypeStruct((1, 256 // CHAN, 256), F32),
    )
    results = pl.pallas_call(
        body,
        out_shape=shapes,
        in_specs=[free] * 5,
        out_specs=(free,) * 5,
        scratch_shapes=[pltpu.VMEM(one.shape, one.dtype) for one in shapes]
        + [
            plane, plane,
            pltpu.VMEM((2, BLK, BLK), BF), pltpu.VMEM((1, 256, 256), BF),
            pltpu.VMEM((3, CH), F32), plane,
            pltpu.VMEM((BATCH, ROWS, EXT), F32), pltpu.VMEM((BATCH, ROWS, EXT), F32),
            plane, plane, plane,
            pltpu.VMEM((2, BATCH, ROWS, EXT), BF),
            pltpu.VMEM((128, 256), F32), pltpu.VMEM((ROWS, 128), F32),
            square, square, plane,
            pltpu.VMEM((7, 256, 256), BF),
            xbuf, xbuf, lbuf, lbuf, lbuf, lbuf, xbuf, xbuf,
            lbuf, lbuf, xbuf, xbuf, xbuf, xbuf, lbuf, lbuf,
            halo, halo, halo, halo,
            pltpu.VMEM((8, 128), F32), pltpu.VMEM((NX, 8, 128), F32),
            pltpu.VMEM((8, 128), F32), pltpu.VMEM((NL, 8, 128), F32),
            pltpu.VMEM((CHAN, 64, 256), F32),
            pltpu.VMEM((2, 64, 256), F32), pltpu.VMEM((64, 256), BF), pltpu.VMEM((64, 256), BF),
            pltpu.VMEM((CHAN, 2, 32, BLK), F32),
            pltpu.VMEM((CHAN, 2, 32, BLK), BF), pltpu.VMEM((CHAN, 2, 32, BLK), BF),
            pltpu.SemaphoreType.DMA((23,)),
            pltpu.SemaphoreType.DMA((23,)),
            pltpu.SemaphoreType.DMA((5,)),
            pltpu.SemaphoreType.DMA((5,)),
        ],
        compiler_params=pltpu.CompilerParams(
            collective_id=0, has_side_effects=True, vmem_limit_bytes=60 * 1024 * 1024
        ),
    )(inputs, first_blocks, second_blocks, kernel, cotangent)
    return pl.pallas_call(
        emit,
        out_shape=shapes,
        in_specs=[free] * 5,
        out_specs=(free,) * 5,
        scratch_shapes=[pltpu.VMEM(one.shape, one.dtype) for one in shapes]
        + [pltpu.SemaphoreType.DMA((2, 7))],
        compiler_params=pltpu.CompilerParams(vmem_limit_bytes=60 * 1024 * 1024),
    )(*results)


def solution(mesh):
    placed = (
        P(None, "chan", "seq"),
        P("seq", None, None),
        P("seq", None, None),
        P(None, "chan"),
        P(None, "chan", "seq"),
    )
    return jax.shard_map(
        shards,
        mesh=mesh,
        in_specs=placed,
        out_specs=(
            P(None, "chan", "seq"),
            P(None, "chan", "seq"),
            P(None, "chan"),
            P("seq", "chan", None),
            P("seq", "chan", None),
        ),
        check_vma=False,
    )
```

```python
import jax
import jax.numpy as jnp
from jax import lax
from jax.experimental import pallas as pl
from jax.experimental.pallas import tpu as pltpu
from jax.sharding import PartitionSpec as P

NX, NL = 8, 16
SEQ, CHAN = NX * NL, 4
BATCH, CH, EXT, BLK = 2, 240, 256, 128
ROWS = 256
MESH = pl.DeviceIdType.MESH
BF, F32 = jnp.bfloat16, jnp.float32
A0, B0, B1, A1, B2, A2, A3, B3 = range(0, 16, 2)
FG, FH, BG, KX, KL, H0, H1 = range(16, 23)


def dot(a, b, ca, cb):
    return lax.dot_general(a, b, (((ca,), (cb,)), ((), ())), preferred_element_type=F32)


def nn(a, b):
    return dot(a, b, 1, 0)


def nt(a, b):
    return dot(a, b, 1, 1)


def tn(a, b):
    return dot(a, b, 0, 0)


def hot(shape, where):
    row = lax.broadcasted_iota(jnp.int32, shape, 0)
    col = lax.broadcasted_iota(jnp.int32, shape, 1)
    return jnp.where(where(row, col), 1.0, 0.0).astype(BF)


def place0(r, c):
    return ((r >> 4) & 1) * 128 + (r & 15) * 8 + (r >> 5) == c


def turn0(r, c):
    return ((r >> 1) & 7) * 32 + (r & 1) * 16 + (r >> 4) == c


def place1(r, c):
    return ((r >> 3) & 1) * 128 + (r >> 4) * 8 + (r & 7) == c


def turn1(r, c):
    return ((r >> 1) & 15) * 16 + (r & 1) * 8 + (r >> 5) == c


def order1(r, c):
    return ((r >> 1) & 7) * 32 + (r >> 4) * 2 + (r & 1) == c


def flip(where):
    return lambda r, c: where(c, r)


def body(
    x_in, f_in, s_in, k_in, c_in,
    mixed_out, igrad_out, kgrad_out, bgrad_out, fgrad_out,
    mixed_ref, igrad_ref, kgrad_ref, bgrad_ref, fgrad_ref,
    xs, cs, fs, sec, kin, xt, gate, total, gat, mon, mgrad, near, kpad, kcol, st, s11, mgr, tables,
    a0s, a0r, b0s, b0r, b1s, b1r, a1s, a1r,
    b2s, b2r, a2s, a2r, a3s, a3r, b3s, b3r,
    h0s, h0r, h1s, h1r,
    kxs, kxr, kls, klr, fgo, fgp, fgs, fgr, bgo, bgs, bgr,
    ssem, rsem, isem, osem,
):
    seq = lax.axis_index("seq")
    chan = lax.axis_index("chan")
    mx = lax.rem(seq, NX)
    ml = lax.div(seq, NX)
    ahead = lax.rem(seq + 1, SEQ)
    behind = lax.rem(seq + SEQ - 1, SEQ)

    def x_peer(d):
        other = lax.rem(mx + d, NX)
        return other, (ml * NX + other, chan)

    def l_peer(d):
        other = lax.rem(ml + d, NL)
        return other, (other * NX + mx, chan)

    def c_peer(d):
        other = lax.rem(chan + d, CHAN)
        return other, (seq, other)

    barrier = pltpu.get_barrier_semaphore()

    def greet(peer, count):
        def step(d, carry):
            pl.semaphore_signal(barrier, inc=1, device_id=peer(d)[1], device_id_type=MESH)
            return carry

        lax.fori_loop(1, count, step, 0)

    loads = [
        pltpu.make_async_copy(c_in, cs.at[:, pl.ds(0, CH), :], isem.at[2]),
        pltpu.make_async_copy(x_in, xs.at[:, pl.ds(0, CH), :], isem.at[0]),
        pltpu.make_async_copy(f_in, fs, isem.at[1]),
        pltpu.make_async_copy(k_in, kin, isem.at[3]),
        pltpu.make_async_copy(s_in, sec, isem.at[4]),
    ]
    for load in loads:
        load.start()
    greet(l_peer, NL)
    greet(x_peer, NX)
    greet(c_peer, CHAN)
    pl.semaphore_signal(barrier, inc=1, device_id=(ahead, chan), device_id_type=MESH)
    pl.semaphore_signal(barrier, inc=1, device_id=(behind, chan), device_id_type=MESH)

    def remote(src, dst, device, sem):
        return pltpu.make_async_remote_copy(
            src_ref=src, dst_ref=dst, send_sem=ssem.at[sem], recv_sem=rsem.at[sem],
            device_id=device, device_id_type=MESH,
        )

    def scatter(send, recv, mine, peer, count, sem):
        def step(i, carry):
            d = count // 2 + lax.div(i + 1, 2) * (2 * lax.rem(i, 2) - 1)
            other, device = peer(d)
            remote(send.at[other], recv.at[mine], device, sem).start()
            return carry

        lax.fori_loop(0, count - 1, step, 0)

    def keep(send, recv, mine):
        recv[mine] = send[mine]

    def spread(send, recv, mine, peer, count, sem):
        def step(i, carry):
            d = count // 2 + lax.div(i + 1, 2) * (2 * lax.rem(i, 2) - 1)
            remote(send, recv.at[mine], peer(d)[1], sem).start()
            return carry

        lax.fori_loop(0, count - 1, step, 0)
        recv[mine] = send[...]

    def arrive(recv, count, sem):
        part = recv.at[pl.ds(0, count - 1)]
        pltpu.make_async_copy(part, part, rsem.at[sem]).wait()

    def sent(send, count, sem):
        part = send.at[pl.ds(0, count - 1)]
        pltpu.make_async_copy(part, part, ssem.at[sem]).wait()

    def flat(ref, b):
        return ref[b].reshape(256, ROWS)

    def over_x(value, send, recv, b, sem):
        send[b] = value.astype(BF).reshape(NX, 32, ROWS)
        scatter(send.at[b], recv.at[b], mx, x_peer, NX, sem + b)
        keep(send.at[b], recv.at[b], mx)

    def over_l(value, send, recv, b, sem):
        send[b] = value.astype(BF).reshape(NL, 16, ROWS)
        scatter(send.at[b], recv.at[b], ml, l_peer, NL, sem + b)
        keep(send.at[b], recv.at[b], ml)

    zero_rows = jnp.zeros((BATCH, ROWS - CH, EXT), BF)
    xs[:, CH:ROWS, :] = zero_rows
    cs[:, CH:ROWS, :] = zero_rows
    kpad[...] = jnp.zeros_like(kpad)
    tables[0] = hot((256, 256), place0)
    tables[1] = hot((256, 256), place1)
    shift1 = hot((EXT, EXT), lambda r, c: r == c + 1)
    shift2 = hot((EXT, EXT), lambda r, c: r == c + 2)

    loads[0].wait()
    head = hot((16, EXT), lambda r, c: (r == c) & (r < 2))
    for b in range(BATCH):
        h0s[b] = nt(head, cs[b]).astype(BF)
    loads[1].wait()
    loads[2].wait()
    p0 = tables[0]
    for b in range(BATCH):
        m0 = nn(xs[b, :, 0:BLK], fs[0]).astype(BF)
        m1 = nn(xs[b, :, BLK:EXT], fs[1]).astype(BF)
        rows = nt(p0[:, 0:BLK], m0) + nt(p0[:, BLK:EXT], m1)
        a0s[b] = rows.astype(BF).reshape(NX, 32, ROWS)

    loads[3].wait()
    kpad[0:3, 0:CH] = kin[...]
    kcol[0:128, :] = kpad[:, 0:128].T
    kcol[128:256, :] = kpad[:, 128:256].T

    def gate_from(lanes, b, cot, near1, near2):
        near[0, b, :, lanes] = near1.astype(BF)
        near[1, b, :, lanes] = near2.astype(BF)
        value = kcol[:, 0:1] * cot.astype(F32) + kcol[:, 1:2] * near1 + kcol[:, 2:3] * near2
        gate[b, :, lanes] = value
        mgrad[b, :, lanes] = (value * xs[b, :, lanes].astype(F32)).astype(BF)

    last = NL - 1
    p1 = tables[1]
    for b in range(BATCH):
        gate_from(slice(0, EXT), b, cs[b], nn(cs[b], shift1), nn(cs[b], shift2))
        b1s[b] = nt(p1, mgrad[b]).astype(BF).reshape(NL, 16, ROWS)

    pl.semaphore_wait(barrier, NX - 1 + NL - 1 + CHAN - 1 + 2)

    halo0 = remote(h0s, h0r, (behind, chan), H0)
    halo0.start()
    for b in range(BATCH):
        scatter(a0s.at[b], a0r.at[b], mx, x_peer, NX, A0 + b)
    for b in range(BATCH):

        def step(i, carry):
            other, device = l_peer(NL // 2 + lax.div(i + 1, 2) * (2 * lax.rem(i, 2) - 1))

            @pl.when(other != last)
            def _():
                remote(b1s.at[b, other], b1r.at[b, ml], device, B1 + b).start()

            return carry

        lax.fori_loop(0, NL - 1, step, 0)
    for b in range(BATCH):
        keep(a0s.at[b], a0r.at[b], mx)

    tables[2] = hot((256, 256), turn0)
    tables[3] = hot((256, 256), flip(turn0))
    tables[4] = hot((256, 256), turn1)
    tables[5] = hot((256, 256), flip(turn1))
    tables[6] = hot((256, 256), order1)
    loads[4].wait()
    eye = hot((256, 256), lambda r, c: r == c)
    second = sec[0]
    st[...] = nt(eye, second).astype(BF)
    back = hot((256, 256), flip(order1))
    s11[...] = nt(nn(back, second).astype(BF), back).astype(BF)

    for b in range(BATCH):
        arrive(a0r.at[b], NX, A0 + b)
        over_l(nn(tables[2], flat(a0r, b)), b0s, b0r, b, B0)

    halo0.wait_recv()
    inside = (seq < SEQ - 1).astype(F32)
    high = slice(BLK, EXT)
    for b in range(BATCH):
        tail = (h0r[b].astype(F32) * inside).astype(BF)
        near1 = near[0, b, :, high].astype(F32)
        near2 = near[1, b, :, high].astype(F32)
        near1 = near1 + tn(tail, hot((16, BLK), lambda r, c: (r == 0) & (c == BLK - 1)))
        near2 = near2 + tn(tail, hot((16, BLK), lambda r, c: (r < 2) & (c == BLK - 2 + r)))
        gate_from(high, b, cs[b, :, high], near1, near2)
        b1s[b, last] = nt(tables[1, 16 * last : 16 * NL], mgrad[b]).astype(BF)

        @pl.when(ml != last)
        def _():
            remote(b1s.at[b, last], b1r.at[b, ml], (last * NX + mx, chan), B1 + b).start()

        keep(b1s.at[b], b1r.at[b], ml)

    for b in range(BATCH):
        xt[b] = nt(eye, xs[b]).astype(BF)
    for b in range(BATCH):
        arrive(b1r.at[b], NL, B1 + b)
        over_x(nn(tables[4], flat(b1r, b)), a1s, a1r, b, A1)
    for b in range(BATCH):
        arrive(b0r.at[b], NL, B0 + b)
        over_l(nn(st[...], flat(b0r, b)), b2s, b2r, b, B2)
    for b in range(BATCH):
        arrive(a1r.at[b], NX, A1 + b)
        over_x(nn(s11[...], flat(a1r, b)), a3s, a3r, b, A3)
    for b in range(BATCH):
        arrive(b2r.at[b], NL, B2 + b)
        over_x(nn(tables[3], flat(b2r, b)), a2s, a2r, b, A2)
        arrive(a3r.at[b], NX, A3 + b)
        over_l(nn(tables[5], flat(a3r, b)), b3s, b3r, b, B3)

    grad = jnp.zeros((256, 256), F32)
    for b in range(BATCH):
        nat = nn(tables[6], flat(a1r, b)).astype(BF)
        grad = grad + nt(flat(b0r, b), nat)
    fgo[...] = grad.reshape(CHAN, 64, 256)
    core = lax.rem(chan, 2)
    half = lax.div(chan, 2)
    for h in range(2):
        remote(fgo.at[2 * h + 1 - core], fgp.at[h], (seq, 2 * half + 1 - core), FG).start()

    prods = [jnp.zeros((ROWS, BLK), F32)] * 3
    for b in range(BATCH):
        arrive(a2r.at[b], NX, A2 + b)
        monarch = tn(flat(a2r, b), tables[0])
        mon[b] = monarch.astype(BF)
        gated = (xs[b].astype(F32) * monarch).astype(BF)
        gat[b] = gated
        gated32 = gated.astype(F32)
        for j in range(3):
            window = cs[b] if j == 0 else near[j - 1, b]
            prod = gated32 * window.astype(F32)
            prods[j] = prods[j] + (prod[:, 0:BLK] + prod[:, BLK:EXT])
    sums = [jnp.sum(prod, axis=1, keepdims=True) for prod in prods]
    lane = lax.broadcasted_iota(jnp.int32, (128, 128), 1)
    wide = jnp.zeros((128, 128), F32)
    for j in range(3):
        wide = jnp.where(lane == j, sums[j][0:128], jnp.where(lane == 3 + j, sums[j][128:256], wide))
    kxs[...] = wide.T[0:8]
    spread(kxs, kxr, mx, x_peer, NX, KX)

    edge = hot((16, EXT), lambda r, c: (r < 2) & (c == EXT - 2 + r))
    for b in range(BATCH):
        h1s[b] = nt(edge, gat[b]).astype(BF)
    halo1 = remote(h1s, h1r, (ahead, chan), H1)
    halo1.start()
    pltpu.make_async_copy(fgp, fgp, rsem.at[FG]).wait()
    fgs[...] = (fgo[2 * (1 - half) + core] + fgp[1 - half]).astype(BF)
    pair = remote(fgs, fgr, (seq, 2 * (1 - half) + core), FH)
    pair.start()

    parts = [jnp.zeros((BLK, BLK), F32)] * 2
    for b in range(BATCH):
        arrive(b3r.at[b], NL, B3 + b)
        mgr[b] = tn(flat(b3r, b), tables[1]).astype(BF)
        for q in range(2):
            lanes = slice(q * BLK, (q + 1) * BLK)
            parts[q] = parts[q] + nn(xt[b, lanes, :], mgr[b, :, lanes])
        if b == 0:
            arrive(kxr, NX, KX)
            kls[...] = sum((kxr[i] for i in range(1, NX)), kxr[0])
            spread(kls, klr, ml, l_peer, NL, KL)
    for q in range(2):
        part = parts[q].reshape(CHAN, 32, BLK)
        for o in range(CHAN):
            bgo[o, q] = part[o]
            bgs[o, q] = part[o].astype(BF)
    scatter(bgs, bgr, chan, c_peer, CHAN, BG)

    far1 = hot((EXT, EXT), lambda r, c: r + 1 == c)
    far2 = hot((EXT, EXT), lambda r, c: r + 2 == c)
    for b in range(BATCH):
        total[b] = (
            kcol[:, 0:1] * gat[b].astype(F32)
            + kcol[:, 1:2] * nn(gat[b], far1)
            + kcol[:, 2:3] * nn(gat[b], far2)
        )
    for q in range(2):
        lanes = slice(q * BLK, (q + 1) * BLK)
        for b in range(BATCH):
            through = nt(mgr[b, :, lanes], fs[q])
            direct = gate[b, :, lanes] * mon[b, :, lanes].astype(F32)
            igrad_ref[b, :, lanes] = (direct + through)[0:CH].astype(BF)

    stores = [
        pltpu.make_async_copy(igrad_ref, igrad_out, osem.at[0]),
        pltpu.make_async_copy(mixed_ref, mixed_out, osem.at[1]),
        pltpu.make_async_copy(fgrad_ref, fgrad_out, osem.at[2]),
        pltpu.make_async_copy(bgrad_ref, bgrad_out, osem.at[3]),
        pltpu.make_async_copy(kgrad_ref, kgrad_out, osem.at[4]),
    ]
    stores[0].start()

    halo1.wait_recv()
    inside = (seq > 0).astype(F32)
    mixed_ref[:, :, high] = total[:, 0:CH, high].astype(BF)
    for b in range(BATCH):
        prior = (h1r[b].astype(F32) * inside).astype(BF)
        edge1 = tn(prior, hot((16, BLK), lambda r, c: (r == 1) & (c == 0)))
        edge2 = tn(prior, hot((16, BLK), lambda r, c: (r < 2) & (r == c)))
        value = total[b, :, 0:BLK] + (kcol[:, 1:2] * edge1 + kcol[:, 2:3] * edge2)
        mixed_ref[b, :, 0:BLK] = value[0:CH].astype(BF)
    stores[1].start()

    pair.wait_recv()
    fgrad_ref[0] = (fgo[chan] + fgp[half]) + fgr[...].astype(F32)
    stores[2].start()
    arrive(bgr, CHAN, BG)
    bgr[chan] = jnp.zeros((2, 32, BLK), BF)
    got = [bgr[i].astype(F32) for i in range(CHAN)]
    bgrad_ref[...] = bgo[chan] + ((got[0] + got[1]) + (got[2] + got[3]))
    stores[3].start()
    arrive(klr, NL, KL)
    whole = sum((klr[i] for i in range(1, NL)), klr[0])
    kgrad_ref[:, 0:128] = whole[0:3]
    kgrad_ref[:, 128:CH] = whole[3:6, 0 : CH - 128]
    stores[4].start()

    halo0.wait_send()
    halo1.wait_send()
    for b in range(BATCH):
        for send, sem in ((a0s, A0), (a1s, A1), (a2s, A2), (a3s, A3)):
            sent(send.at[b], NX, sem + b)
        for send, sem in ((b0s, B0), (b1s, B1), (b2s, B2), (b3s, B3)):
            sent(send.at[b], NL, sem + b)
    pltpu.make_async_copy(fgp, fgp, ssem.at[FG]).wait()
    pair.wait_send()
    sent(bgs, CHAN, BG)
    sent(kxr, NX, KX)
    sent(klr, NL, KL)
    for store in stores:
        store.wait()


def emit(*refs):
    ins, outs, held, sem = refs[0:5], refs[5:10], refs[10:15], refs[15]
    parts = [(0, 0), (1, 0), (0, 1), (1, 1), (4, 0), (3, 0), (2, 0)]

    def piece(ref, i, b):
        return ref.at[b] if i < 2 else ref

    loads, stores = [], []
    for n, (i, b) in enumerate(parts):
        source, stage, target = piece(ins[i], i, b), piece(held[i], i, b), piece(outs[i], i, b)
        loads.append(pltpu.make_async_copy(source, stage, sem.at[0, n]))
        stores.append(pltpu.make_async_copy(stage, target, sem.at[1, n]))
    for load in loads:
        load.start()
    for load, store in zip(loads, stores):
        load.wait()
        store.start()
    for store in stores:
        store.wait()


def shards(inputs, first_blocks, second_blocks, kernel, cotangent):
    free = pl.BlockSpec(memory_space=pl.ANY)
    xbuf = pltpu.VMEM((BATCH, NX, 32, ROWS), BF)
    lbuf = pltpu.VMEM((BATCH, NL, 16, ROWS), BF)
    halo = pltpu.VMEM((BATCH, 16, ROWS), BF)
    plane = pltpu.VMEM((BATCH, ROWS, EXT), BF)
    square = pltpu.VMEM((256, 256), BF)
    shapes = (
        jax.ShapeDtypeStruct((BATCH, CH, EXT), BF),
        jax.ShapeDtypeStruct((BATCH, CH, EXT), BF),
        jax.ShapeDtypeStruct((3, CH), F32),
        jax.ShapeDtypeStruct((2, BLK // CHAN, BLK), F32),
        jax.ShapeDtypeStruct((1, 256 // CHAN, 256), F32),
    )
    results = pl.pallas_call(
        body,
        out_shape=shapes,
        in_specs=[free] * 5,
        out_specs=(free,) * 5,
        scratch_shapes=[pltpu.VMEM(one.shape, one.dtype) for one in shapes]
        + [
            plane, plane,
            pltpu.VMEM((2, BLK, BLK), BF), pltpu.VMEM((1, 256, 256), BF),
            pltpu.VMEM((3, CH), F32), plane,
            pltpu.VMEM((BATCH, ROWS, EXT), F32), pltpu.VMEM((BATCH, ROWS, EXT), F32),
            plane, plane, plane,
            pltpu.VMEM((2, BATCH, ROWS, EXT), BF),
            pltpu.VMEM((128, 256), F32), pltpu.VMEM((ROWS, 128), F32),
            square, square, plane,
            pltpu.VMEM((7, 256, 256), BF),
            xbuf, xbuf, lbuf, lbuf, lbuf, lbuf, xbuf, xbuf,
            lbuf, lbuf, xbuf, xbuf, xbuf, xbuf, lbuf, lbuf,
            halo, halo, halo, halo,
            pltpu.VMEM((8, 128), F32), pltpu.VMEM((NX, 8, 128), F32),
            pltpu.VMEM((8, 128), F32), pltpu.VMEM((NL, 8, 128), F32),
            pltpu.VMEM((CHAN, 64, 256), F32),
            pltpu.VMEM((2, 64, 256), F32), pltpu.VMEM((64, 256), BF), pltpu.VMEM((64, 256), BF),
            pltpu.VMEM((CHAN, 2, 32, BLK), F32),
            pltpu.VMEM((CHAN, 2, 32, BLK), BF), pltpu.VMEM((CHAN, 2, 32, BLK), BF),
            pltpu.SemaphoreType.DMA((23,)),
            pltpu.SemaphoreType.DMA((23,)),
            pltpu.SemaphoreType.DMA((5,)),
            pltpu.SemaphoreType.DMA((5,)),
        ],
        compiler_params=pltpu.CompilerParams(
            collective_id=0, has_side_effects=True, vmem_limit_bytes=60 * 1024 * 1024
        ),
    )(inputs, first_blocks, second_blocks, kernel, cotangent)
    return pl.pallas_call(
        emit,
        out_shape=shapes,
        in_specs=[free] * 5,
        out_specs=(free,) * 5,
        scratch_shapes=[pltpu.VMEM(one.shape, one.dtype) for one in shapes]
        + [pltpu.SemaphoreType.DMA((2, 7))],
        compiler_params=pltpu.CompilerParams(vmem_limit_bytes=60 * 1024 * 1024),
    )(*results)


def solution(mesh):
    placed = (
        P(None, "chan", "seq"),
        P("seq", None, None),
        P("seq", None, None),
        P(None, "chan"),
        P(None, "chan", "seq"),
    )
    return jax.shard_map(
        shards,
        mesh=mesh,
        in_specs=placed,
        out_specs=(
            P(None, "chan", "seq"),
            P(None, "chan", "seq"),
            P(None, "chan"),
            P("seq", "chan", None),
            P("seq", "chan", None),
        ),
        check_vma=False,
    )
```
